32 devices in a mesh: domain: 8 (over z, x), group: 4 (over y, core).
Axes of the slice: x: 2, y: 2, z: 4, core: 2. Of those that a mesh axis runs over, the one named last changes fastest.
Arguments:
- centers: float32 [2048, 3], P(('domain', 'group')), may hold values from -24 to 24
- offsets: float32 [2048, 3, 144], P(('domain', 'group')), may hold values from -6 to 6
- density: float32 [2048, 3, 144], P(('domain', 'group')), may hold values from -6 to 6
- area: float32 [2048, 144], P(('domain', 'group')), may hold values from 0.03 to 0.3
- upsample: float32 [544, 144], replicated
- self_operator: float32 [144, 144], replicated, may hold values from -0.5 to 0.5
- near_sources: int32 [2048, 4], P(('domain', 'group')), may hold values from 0 to 2047, as said below
- near_counts: int32 [2048], P(('domain', 'group')), may hold values from 1 to 4, as said below
- leaf_slot: int32 [2048], P(('domain', 'group')), may hold values from 0 to 4095, as said below
- leaf_list: int32 [256, 8], P(('domain', 'group')), may hold values from 0 to 255
Outputs:
- velocity: float32 [2048, 3, 144], P(('domain', 'group'))
The draws below stay inside these ranges and needn't reach their ends.
Inputs may be any that keep to these rules, and one draw needn't show every extreme that they name: `near_sources`: each near source lies in the target's own domain or in one of the two adjacent domains of 2048 / 8 vesicles, and is never the target itself; slots past the count hold valid indices too. `near_counts`: the first vesicle of every device has 4 live slots. `leaf_slot`: no two vesicles share a slot, and a vesicle's slot lies in a leaf block of a device of its own domain.
All inputs are finite; a program needn't handle non-finite values.
Results may differ from the reference program's by a relative error of at most 0.00014.
Values sent between devices are 32-bit elements; how exact they have to be, the bound alone decides.
No kernel may reach another device: no remote copies, remote signals or barrier semaphores. Data moves between devices by JAX's collectives and lax.ppermute only.
A program may use at most 128 MiB of HBM per device.

```python
import math
import jax
import jax.numpy as jnp
from jax import lax

P_SIZE = 144
Q = 544
V_DEV = 64
K_MAX = 4
LEAF_DEV = 8
LEAF_CAP = 16
L_NBR = 8
VESICLES = 2048
LEAVES = 256
N_DOMAIN = 8
N_GROUP = 4


def draw_upsample(key, part):
    rows = lax.broadcasted_iota(jnp.int32, (Q, P_SIZE), 0)
    cols = lax.broadcasted_iota(jnp.int32, (Q, P_SIZE), 1)
    nearest = (cols == rows * P_SIZE // Q).astype(jnp.float32)
    noise = jax.random.normal(key, (Q, P_SIZE), jnp.float32)
    return nearest + 0.05 * (noise - jnp.roll(noise, 1, axis=1))


def draw_near_sources(key, part):
    rows = jnp.arange(VESICLES, dtype=jnp.int32)
    home = rows // (N_GROUP * V_DEV)
    key_step, key_group, key_local = jax.random.split(key, 3)
    step = jax.random.randint(key_step, (VESICLES, K_MAX), -1, 2)
    domain = jnp.clip(home[:, None] + step, 0, N_DOMAIN - 1)
    group = jax.random.randint(key_group, (VESICLES, K_MAX), 0, N_GROUP)
    local = jax.random.randint(key_local, (VESICLES, K_MAX), 0, V_DEV)
    source = (domain * N_GROUP + group) * V_DEV + local
    local = jnp.where(source == rows[:, None], (local + 1) % V_DEV, local)
    source = (domain * N_GROUP + group) * V_DEV + local
    column = lax.broadcasted_iota(jnp.int32, (VESICLES, K_MAX), 1)
    top_row = (rows[:, None] == VESICLES - 2) & (column == 0)
    low_row = (rows[:, None] == 1) & (column == 0)
    source = jnp.where(top_row, VESICLES - 1, source)
    source = jnp.where(low_row, 0, source)
    return source.astype(jnp.int32)


def draw_near_counts(key, part):
    counts = jax.random.randint(key, (VESICLES,), 1, K_MAX + 1)
    first = jnp.arange(VESICLES, dtype=jnp.int32) % V_DEV == 0
    return jnp.where(first, K_MAX, counts).astype(jnp.int32)


def draw_leaf_slot(key, part):
    per_domain = N_GROUP * LEAF_DEV * LEAF_CAP
    used = N_GROUP * V_DEV
    keys = jax.random.split(key, N_DOMAIN)

    def one_domain(sub_key, index):
        key_pick, key_order = jax.random.split(sub_key)
        middle = 1 + jax.random.permutation(key_pick, per_domain - 2)[:used - 2]
        ends = jnp.array([0, per_domain - 1], dtype=jnp.int32)
        chosen = jnp.concatenate([ends, middle.astype(jnp.int32)])
        order = jax.random.permutation(key_order, used)
        return index * per_domain + chosen[order]
    slots = jax.vmap(one_domain)(keys, jnp.arange(N_DOMAIN, dtype=jnp.int32))
    return slots.reshape(VESICLES).astype(jnp.int32)


def plant(entries, rng, least, largest):
    extent = entries.shape
    index_at = [jax.random.randint(jax.random.fold_in(rng, axis), (), 0, extent[axis]) for axis in range(len(extent))]
    entries = entries.at[tuple(index_at)].set(least)
    longest = extent.index(max(extent))
    index_at[longest] = (index_at[longest] + 1) % extent[longest]
    return entries.at[tuple(index_at)].set(largest)


def block_scale(rng, extent, cuts, smallest, top_value):
    factor_of = 1.0
    for position, parts in cuts:
        steps = jax.random.uniform(jax.random.fold_in(jax.random.fold_in(rng, 6), position), (parts,), jnp.float32, smallest / len(cuts), top_value / len(cuts))
        factor_of = factor_of * jnp.repeat(jnp.exp(steps), extent[position] // parts).reshape((-1,) + (1,) * (len(extent) - 1 - position))
    return factor_of


def bell_draw(rng, shape, scale, reach, shards=(), kind=jnp.bfloat16):
    loudness = block_scale(rng, shape, shards, -0.22, 0.18) if shards else 1.0
    drawn = jax.random.normal(rng, shape, jnp.float32) * scale * loudness
    return jnp.minimum(jnp.maximum(drawn, -reach), reach).astype(kind)


def setup_inputs(seed: int = 0) -> dict:
    splits = jax.random.split(jax.random.key(seed), 11)
    return {
        "centers": bell_draw(splits[0], (VESICLES, 3), 4.0, 24.0, ((0, 32),), jnp.float32),
        "offsets": bell_draw(splits[1], (VESICLES, 3, P_SIZE), 1.0, 6.0, ((0, 32),), jnp.float32),
        "density": bell_draw(splits[2], (VESICLES, 3, P_SIZE), 1.0, 6.0, ((0, 32),), jnp.float32),
        "area": jnp.clip(jnp.exp(math.log(0.3) - 2.3025852 * jax.random.uniform(splits[3], (VESICLES, P_SIZE), jnp.float32) ** block_scale(splits[3], (VESICLES, P_SIZE), ((0, 32),), -0.2, 0.2)), 0.03, 0.3),
        "upsample": draw_upsample(jax.random.fold_in(splits[10], 71), 0),
        "self_operator": bell_draw(splits[5], (P_SIZE, P_SIZE), P_SIZE ** -0.5, 0.5, (), jnp.float32),
        "near_sources": draw_near_sources(jax.random.fold_in(splits[10], 71), 0),
        "near_counts": draw_near_counts(jax.random.fold_in(splits[10], 71), 0),
        "leaf_slot": draw_leaf_slot(jax.random.fold_in(splits[10], 71), 0),
        "leaf_list": plant(jax.random.randint(splits[9], (LEAVES, L_NBR), 0, LEAVES), jax.random.fold_in(splits[9], 1), 0, LEAVES - 1).astype(jnp.int32),
    }


BLOB2 = 0.25

def stokes(rel, force):
    dist = lax.optimization_barrier(jnp.sum(rel * rel, axis=0)) + BLOB2
    inverse = 1.0 / (dist * jnp.sqrt(dist))
    project = lax.optimization_barrier(jnp.sum(rel * force, axis=0))
    return lax.optimization_barrier(jnp.sum(inverse * ((dist + BLOB2) * force + project * rel), axis=-1))

def near_block(targets, sources):
    rel = targets[:, :, None, :, None] - sources[:3, :, :, None, :]
    return lax.optimization_barrier(jnp.sum(stokes(rel, sources[3:, :, :, None, :]), axis=2))

def reference(centers, offsets, density, area, upsample, self_operator, near_sources, near_counts, leaf_slot, leaf_list):
    highest = lax.Precision.HIGHEST
    grid = offsets + centers[:, :, None]
    weighted = density * area[:, None, :]
    coarse = jnp.concatenate([grid, weighted], axis=1)
    fine = jnp.einsum('qp,vcp->vcq', upsample, coarse, precision=highest)
    self_term = jnp.einsum('ip,vcp->vci', self_operator, density, precision=highest)
    live = (jnp.arange(K_MAX, dtype=jnp.int32)[None, :] < near_counts[:, None]).astype(jnp.float32)
    block = math.gcd(VESICLES, 16)
    blocks = VESICLES // block

    def one_block(items):
        targets, spots, mask = items
        picked = jnp.transpose(fine[spots], (2, 0, 1, 3))
        picked = jnp.concatenate([picked[:3], picked[3:] * mask[None, :, :, None]], axis=0)
        return near_block(jnp.transpose(targets, (1, 0, 2)), picked)
    near = lax.map(one_block, (grid.reshape(blocks, block, 3, P_SIZE), near_sources.reshape(blocks, block, K_MAX), live.reshape(blocks, block, K_MAX)))
    near = jnp.transpose(near, (0, 2, 1, 3)).reshape(VESICLES, 3, P_SIZE)
    total = lax.optimization_barrier(jnp.sum(weighted, axis=2))
    slots_all = LEAVES * LEAF_CAP
    slot_centers = jnp.zeros((slots_all, 3), jnp.float32).at[leaf_slot].set(centers)
    slot_forces = jnp.zeros((slots_all, 3), jnp.float32).at[leaf_slot].set(total)
    lists = leaf_list[leaf_slot // LEAF_CAP]
    spots = (lists[:, :, None] * LEAF_CAP + jnp.arange(LEAF_CAP, dtype=jnp.int32)[None, None, :]).reshape(VESICLES, L_NBR * LEAF_CAP)
    rel = jnp.transpose(centers)[:, :, None] - jnp.transpose(slot_centers[spots], (2, 0, 1))
    far = stokes(rel, jnp.transpose(slot_forces[spots], (2, 0, 1)))
    return self_term + near + jnp.transpose(far)[:, :, None]
```

```python
import functools

import jax
import jax.numpy as jnp
from jax import lax
from jax.experimental import pallas as pl
from jax.experimental.pallas import tpu as pltpu
from jax.sharding import PartitionSpec as P

LEAF_CAP = 16
EPS = 0.5
UNITS = 4
BATCH = 32
PARTS = 6
F32 = jnp.float32
BF16 = jnp.bfloat16
HIGHEST = lax.Precision.HIGHEST
VMEM_SPEC = pl.BlockSpec(memory_space=pltpu.VMEM)
SMEM_SPEC = pl.BlockSpec(memory_space=pltpu.SMEM)


def params(mib):
    return pltpu.CompilerParams(vmem_limit_bytes=mib << 20)


def iota(shape, dim):
    return lax.broadcasted_iota(jnp.int32, shape, dim)


def split3(value):
    high = value.astype(BF16).astype(F32)
    rest = value - high
    mid = rest.astype(BF16).astype(F32)
    return high, mid, rest - mid


def stack_left(value, axis):
    h, m, l = split3(value)
    return jnp.concatenate([h, m, l, h, m, h], axis=axis)


def stack_right(value, axis):
    h, m, l = split3(value)
    return jnp.concatenate([h, h, h, m, m, l], axis=axis)


def dot_nt(a, b, precision=None):
    return lax.dot_general(
        a, b, (((1,), (1,)), ((), ())), precision=precision, preferred_element_type=F32
    )


def column(row):
    n = row.shape[1]
    eye = iota((n, n), 0) == iota((n, n), 1)
    return jnp.sum(jnp.where(eye, row, jnp.zeros_like(row)), axis=1, keepdims=True)


def as_row(col):
    n = col.shape[0]
    eye = iota((n, n), 0) == iota((n, n), 1)
    return jnp.sum(jnp.where(eye, col, jnp.zeros_like(col)), axis=0, keepdims=True)


def pack_kernel(cen_ref, off_ref, den_ref, area_ref, leaf_ref, list_ref, tile_ref, load_ref):
    rows, points = area_ref.shape
    area = area_ref[...]
    tail = points - 128
    tails = []
    lines = []
    for c in range(3):
        grid = off_ref[c] + column(cen_ref[c : c + 1, :])
        tile_ref[pl.ds(c, rows, 8), :] = grid[:, :128]
        tails.append(grid[:, 128:])
    for c in range(3):
        weighted = den_ref[c] * area
        tile_ref[pl.ds(3 + c, rows, 8), :] = weighted[:, :128]
        tails.append(weighted[:, 128:])
        lines.append(as_row(jnp.sum(weighted, axis=1, keepdims=True)))
    tails.append(jnp.zeros((rows, 128 - 6 * tail), F32))
    tile_ref[pl.ds(6, rows, 8), :] = jnp.concatenate(tails, axis=1)
    tile_ref[pl.ds(7, rows, 8), :] = jnp.zeros((rows, 128), F32)
    leaf = (leaf_ref[...] // LEAF_CAP).astype(F32)
    block = jnp.concatenate([cen_ref[...]] + lines + [leaf, jnp.zeros((1, rows), F32)], axis=0)
    lists = list_ref[...].astype(F32)
    rest = 128 - rows - lists.shape[1]
    load_ref[...] = jnp.concatenate([block, lists, jnp.zeros((8, rest), F32)], axis=1)


def pack(cen, off, den, area, leaf, lists):
    rows = area.shape[0]
    return pl.pallas_call(
        pack_kernel,
        out_shape=(
            jax.ShapeDtypeStruct((8 * rows, 128), F32),
            jax.ShapeDtypeStruct((8, 128), F32),
        ),
        in_specs=[VMEM_SPEC] * 6,
        out_specs=(VMEM_SPEC, VMEM_SPEC),
        compiler_params=params(32),
        name="pack",
    )(cen, off, den, area, leaf, lists)


def left_kernel(groups, place_ref, src_ref, cnt_ref, off_ref, den_ref, op_ref, up_ref,
                left_ref, self_ref, upw_ref, t1, s1, k1, t2, s2, k2, n_ref):
    _, rows, points = off_ref.shape
    slots = src_ref.shape[1]
    domain = place_ref[0]
    group = place_ref[1]

    def each_target(t, state):
        live = cnt_ref[t]
        a, b = state
        for k in range(slots):
            src = src_ref[t, k]
            step = src // (groups * rows) - domain
            turn = jnp.bitwise_xor(src // rows % groups, group)
            near = step == 0
            base = turn * rows + src % rows
            is_live = k < live
            t1[a] = t
            s1[a] = base
            k1[a] = k
            t2[b] = t
            s2[b] = base + jnp.where(step > 0, groups * rows, 0)
            k2[b] = k
            a += jnp.where(jnp.logical_and(is_live, near), 1, 0)
            b += jnp.where(jnp.logical_and(is_live, jnp.logical_not(near)), 1, 0)
        return a, b

    a, b = lax.fori_loop(0, rows, each_target, (0, 0))
    n_ref[0] = a
    n_ref[1] = b

    def pad_one(i, _):
        t1[a + i] = 0
        k1[a + i] = 0
        s1[a + i] = groups * rows
        t2[b + i] = 0
        k2[b + i] = 0
        s2[b + i] = 2 * groups * rows
        return 0

    lax.fori_loop(0, BATCH + 2 * UNITS, pad_one, 0)

    eye = (iota((points, points), 0) == iota((points, points), 1)).astype(BF16)

    def one_left(t, _):
        x = [off_ref[c, pl.ds(t, 1), :] * (1.0 / EPS) for c in range(3)]
        xx = x[0] * x[0] + x[1] * x[1] + x[2] * x[2]
        one = jnp.ones_like(xx)
        zero = jnp.zeros_like(xx)
        cases = [[xx]]
        for c in range(3):
            cases.append([xx + x[c] * x[c], x[c] * x[(c + 1) % 3], x[c] * x[(c + 2) % 3]])
        for o, extra in enumerate(cases):
            lines = x + [one] + extra
            lines += [zero] * (8 - len(lines))
            stacked = stack_left(jnp.concatenate(lines, axis=0), 0).astype(BF16)
            left_ref[t, o, :, : 8 * PARTS] = dot_nt(eye, stacked).astype(BF16)
        return 0

    lax.fori_loop(0, rows, one_left, 0)

    for c in range(3):
        self_ref[c] = dot_nt(den_ref[c], op_ref[...], HIGHEST)

    fine = up_ref.shape[1]
    full = fine // 128 * 128
    rest = fine - full
    tail = points - 128
    up = up_ref[...]
    wide = jnp.concatenate([up[:, :full]] + [up[:, full:]] * (128 // rest), axis=1)
    weights = jnp.concatenate(
        [wide[:128]] + [wide[128:]] * 6 + [jnp.zeros((128 - 6 * tail, full + 128), F32)], axis=0
    )
    for i, part in enumerate(split3(weights)):
        upw_ref[i] = part.astype(BF16)


def left(groups, place, src, cnt, off, den, op, up_t):
    rows, slots = src.shape
    points = off.shape[2]
    fine = up_t.shape[1]
    size = rows * slots + BATCH + 2 * UNITS
    ints = jax.ShapeDtypeStruct((size,), jnp.int32)
    return pl.pallas_call(
        functools.partial(left_kernel, groups),
        out_shape=(
            jax.ShapeDtypeStruct((rows, 4, points, 128), BF16),
            jax.ShapeDtypeStruct((3, rows, points), F32),
            jax.ShapeDtypeStruct((3, 256, fine // 128 * 128 + 128), BF16),
        )
        + (ints,) * 6
        + (jax.ShapeDtypeStruct((2,), jnp.int32),),
        in_specs=[SMEM_SPEC] * 3 + [VMEM_SPEC] * 4,
        out_specs=(VMEM_SPEC,) * 3 + (SMEM_SPEC,) * 7,
        compiler_params=params(40),
        name="left",
    )(place, src, cnt, off, den, op, up_t)


def right(tile):
    width = tile.shape[1]
    sub = iota((8, width), 0)
    y = [tile[c : c + 1] for c in range(3)]
    f = [tile[3 + c : 4 + c] for c in range(3)]
    yy = y[0] * y[0] + y[1] * y[1] + y[2] * y[2]
    yf = y[0] * f[0] + y[1] * f[1] + y[2] * f[2]
    zero = jnp.zeros_like(yy)
    one = jnp.ones_like(yy)
    points = jnp.concatenate([y[0], y[1], y[2], -0.5 * yy - 1.0] + [zero] * 4, axis=0)
    forces = jnp.concatenate([f[0], f[1], f[2], -yf] + [zero] * 4, axis=0)
    outs = [
        jnp.concatenate(
            [-2.0 * y[0], -2.0 * y[1], -2.0 * y[2], yy + 1.0, one] + [zero] * 3, axis=0
        )
    ]
    for c in range(3):
        extra = jnp.concatenate([zero] * 4 + [f[c], f[(c + 1) % 3], f[(c + 2) % 3], zero], axis=0)
        extra = jnp.where(sub == c, -yf, extra)
        outs.append(extra - 2.0 * f[c] * points - y[c] * forces)
    return [stack_right(v, 0).astype(BF16) for v in outs]


def shifted(tile, center):
    sub = iota(tile.shape, 0)
    shift = jnp.where(sub == 0, center[0], jnp.where(sub == 1, center[1], center[2]))
    return jnp.where(sub < 3, (tile - shift) * (1.0 / EPS), tile)


def evaluate(lefts, rights, width):
    sums = [0.0, 0.0, 0.0]
    total = rights[0].shape[1]
    for start in range(0, total, width):
        cut = slice(start, start + width)
        dist, *tops = [
            jnp.dot(lefts[o], rights[o][:, cut], preferred_element_type=F32) for o in range(4)
        ]
        u = lax.rsqrt(dist)
        w = u * u * u
        for c in range(3):
            product = w * tops[c]
            for j in range(0, width, 128):
                sums[c] = sums[c] + product[:, j : j + 128]
    return [jnp.sum(s, axis=1, keepdims=True) for s in sums]


def near_kernel(n_blocks, which, last, *refs):
    t_ref, s_ref, k_ref, n_ref, cen_ref = refs[:5]
    refs = refs[5:]
    blocks = refs[:n_blocks]
    left_ref, upw_ref = refs[n_blocks : n_blocks + 2]
    refs = refs[n_blocks + 2 :]
    if last:
        cols_in, tail_in, self_ref, far_ref = refs[:4]
        out_ref = refs[4]
        refs = refs[5:]
    else:
        cols_out, tail_out = refs[:2]
        refs = refs[2:]
    if last:
        pool, fine, tails, cols, rows_a, rows_b, wa, wb = refs
    else:
        pool, fine, rows_a, rows_b, wa, wb = refs
        cols, tails = cols_out, tail_out

    rows = left_ref.shape[0]
    points = left_ref.shape[2]
    full = upw_ref.shape[2] - 128
    held = blocks[0].shape[0]
    for i, block in enumerate(blocks):
        pool[pl.ds(i * held, held)] = block[...]
    pool[n_blocks * held] = jnp.zeros((8, 128), F32)
    if last:
        cols[...] = cols_in[...]
        tails[...] = tail_in[...]
    else:
        cols[...] = jnp.zeros_like(cols)
        tails[...] = jnp.zeros_like(tails)

    n = n_ref[which]
    sub = iota((8, 128), 0)
    lane = iota((8, 128), 1)
    own_lanes = lane // (points - 128) == sub
    k_lane = lane // 32

    def upsample(b, _):
        for j in range(BATCH):
            tile = pool[s_ref[b * BATCH + j]]
            rows_a[pl.ds(8 * j, 8), :] = jnp.where(sub < 6, tile, 0.0)
            rows_b[pl.ds(8 * j, 8), :] = jnp.where(
                jnp.logical_and(own_lanes, sub < 6), tile[6:7, :], 0.0
            )
        value = jnp.concatenate([rows_a[...], rows_b[...]], axis=1)
        h, m, l = [v.astype(BF16) for v in split3(value)]
        uh, um, ul = upw_ref[0], upw_ref[1], upw_ref[2]
        out = None
        for a, w in ((h, uh), (h, um), (m, uh), (h, ul), (l, uh), (m, um)):
            term = jnp.dot(a, w, preferred_element_type=F32)
            out = term if out is None else out + term
        out = out.reshape(BATCH, 8, full + 128)
        fine[pl.ds(b * BATCH, BATCH)] = out[:, :, :full]
        for j in range(BATCH):
            i = b * BATCH + j
            t = t_ref[i]
            mine = jnp.logical_and(k_lane == k_ref[i], i < n)
            tails[t] = jnp.where(mine, out[j, :, full:], tails[t])
        return 0

    lax.fori_loop(0, (n + BATCH - 1) // BATCH, upsample, 0)

    lane_p = iota((points, 128), 1)

    def add_cols(t, sums):
        for c in range(3):
            cols[c] += jnp.where(lane_p == t, sums[c], 0.0)

    def center_of(t):
        return [cen_ref[c, t] for c in range(3)]

    def build(i, w):
        for j in range(UNITS):
            u = i * UNITS + j
            for o, v in enumerate(right(shifted(fine[u], center_of(t_ref[u])))):
                w[j, o] = v

    def main(i, w):
        found = []
        for j in range(UNITS):
            t = t_ref[i * UNITS + j]
            lefts = [left_ref[t, o, :, : 8 * PARTS] for o in range(4)]
            rights = [w[j, o] for o in range(4)]
            found.append((t, evaluate(lefts, rights, 256)))
        for c in range(3):
            value = cols[c]
            for t, sums in found:
                value = value + jnp.where(lane_p == t, sums[c], 0.0)
            cols[c] = value

    build(0, wa)

    def two(i, _):
        build(2 * i + 1, wb)
        main(2 * i, wa)
        build(2 * i + 2, wa)
        main(2 * i + 1, wb)
        return 0

    lax.fori_loop(0, (n + 2 * UNITS - 1) // (2 * UNITS), two, 0)

    if last:
        each = 4

        def tail_pass(i, _):
            found = []
            for j in range(each):
                t = i * each + j
                lefts = [left_ref[t, o, :, : 8 * PARTS] for o in range(4)]
                found.append((t, evaluate(lefts, right(shifted(tails[t], center_of(t))), 128)))
            for c in range(3):
                value = cols[c]
                for t, sums in found:
                    value = value + jnp.where(lane_p == t, sums[c], 0.0)
                cols[c] = value
            return 0

        lax.fori_loop(0, rows // each, tail_pass, 0)
        for c in range(3):
            turned = jnp.transpose(cols[c])[:rows]
            out_ref[c] = turned * (1.0 / EPS) + self_ref[c] + far_ref[c][:, :1]


def near(which, last, blocks, lists, counts, cen, lefts, upw, extra):
    t, s, k = lists
    rows, _, points, _ = lefts.shape
    full = upw.shape[2] - 128
    held = blocks[0].shape[0]
    n_blocks = len(blocks)
    size = t.shape[0]
    cols = jax.ShapeDtypeStruct((3, points, 128), F32)
    tails = jax.ShapeDtypeStruct((rows, 8, 128), F32)
    if last:
        out_shape = jax.ShapeDtypeStruct((3, rows, points), F32)
        out_specs = VMEM_SPEC
    else:
        out_shape = (cols, tails)
        out_specs = (VMEM_SPEC, VMEM_SPEC)
    scratch = [
        pltpu.VMEM((n_blocks * held + 1, 8, 128), F32),
        pltpu.VMEM((size, 8, full), F32),
    ]
    if last:
        scratch += [pltpu.VMEM(tails.shape, F32), pltpu.VMEM(cols.shape, F32)]
    scratch += [pltpu.VMEM((8 * BATCH, 128), F32)] * 2
    scratch += [pltpu.VMEM((UNITS, 4, 8 * PARTS, full), BF16)] * 2
    return pl.pallas_call(
        functools.partial(near_kernel, n_blocks, which, last),
        out_shape=out_shape,
        in_specs=[SMEM_SPEC] * 5 + [VMEM_SPEC] * (n_blocks + 2 + len(extra)),
        out_specs=out_specs,
        scratch_shapes=scratch,
        compiler_params=params(56),
        name="near_last" if last else "near_own",
    )(t, s, k, counts, cen, *blocks, lefts, upw, *extra)


def far_kernel(groups, place_ref, mine_ref, all_ref, far_ref):
    rows = far_ref.shape[1]
    devices = all_ref.shape[0]
    domain = place_ref[0]
    mine = mine_ref[...]
    block = mine[:, :rows]
    center = [column(block[c : c + 1]) for c in range(3)]
    leaf = column(block[6:7])
    leaves = jnp.concatenate(
        [all_ref[domain * groups + g][:, rows : rows + 8] for g in range(groups)], axis=0
    )
    count = groups * 8
    first = (domain * count).astype(F32)
    hot = (leaf - first == iota((rows, count), 1).astype(F32)).astype(F32)
    lists = jnp.dot(hot, leaves, precision=HIGHEST, preferred_element_type=F32)
    lists = jnp.round(lists)
    wanted = [lists[:, k : k + 1] for k in range(8)]
    lane = iota((8, 128), 1)

    def one(i, sums):
        both = jnp.where(lane < 64, all_ref[2 * i], pltpu.roll(all_ref[2 * i + 1], 64, 1))
        rel = [center[c] - both[c : c + 1] for c in range(3)]
        force = [both[3 + c : 4 + c] for c in range(3)]
        source = both[6:7]
        times = jnp.zeros((rows, 128), F32)
        for k in range(8):
            times = times + jnp.where(wanted[k] == source, 1.0, 0.0)
        dist = rel[0] * rel[0] + rel[1] * rel[1] + rel[2] * rel[2] + EPS * EPS
        u = lax.rsqrt(dist)
        u3 = u * u * u * times
        near_part = (dist + EPS * EPS) * u3
        project = (rel[0] * force[0] + rel[1] * force[1] + rel[2] * force[2]) * u3
        return [sums[c] + near_part * force[c] + project * rel[c] for c in range(3)]

    sums = lax.fori_loop(0, devices // 2, one, [jnp.zeros((rows, 128), F32)] * 3)
    for c in range(3):
        far_ref[c] = jnp.broadcast_to(jnp.sum(sums[c], axis=1, keepdims=True), (rows, 128))


def far_field(groups, place, mine, everything, rows):
    return pl.pallas_call(
        functools.partial(far_kernel, groups),
        out_shape=jax.ShapeDtypeStruct((3, rows, 128), F32),
        in_specs=[SMEM_SPEC, VMEM_SPEC, VMEM_SPEC],
        out_specs=VMEM_SPEC,
        compiler_params=params(32),
        name="far",
    )(place, mine, everything)


def swap(x, axis, bit):
    return lax.ppermute(x, axis, [(i, i ^ bit) for i in range(lax.axis_size(axis))])


def bits(n):
    found = []
    bit = 1
    while bit < n:
        found.append(bit)
        bit *= 2
    return found


def shards(
    centers,
    offsets,
    density,
    area,
    upsample,
    self_operator,
    near_sources,
    near_counts,
    leaf_slot,
    leaf_list,
):
    rows = centers.shape[0]
    groups = lax.axis_size("group")
    domains = lax.axis_size("domain")
    place = jnp.stack([lax.axis_index("domain"), lax.axis_index("group")]).astype(jnp.int32)
    cen = centers.T
    off = jnp.transpose(offsets, (1, 0, 2))
    den = jnp.transpose(density, (1, 0, 2))
    tiles, load = pack(cen, off, den, area, leaf_slot[None, :], leaf_list)
    tiles = tiles.reshape(rows, 8, 128)
    ends = domains - 1
    above = lax.ppermute(tiles, "domain", [(i + 1, i) for i in range(ends)])
    below = lax.ppermute(tiles, "domain", [(i, i + 1) for i in range(ends)])
    own = [tiles]
    sides = [[below], [above]]
    for bit in reversed(bits(groups)):
        own = own + [swap(v, "group", bit) for v in own]
        sides = [side + [swap(v, "group", bit) for v in side] for side in sides]
    order = [0]
    for bit in reversed(bits(groups)):
        order = order + [i ^ bit for i in order]
    rank = [order.index(i) for i in range(groups)]
    own = [own[i] for i in rank]
    sides = [[side[i] for i in rank] for side in sides]

    everything = load[None]
    for axis, size in (("domain", domains), ("group", groups)):
        for bit in reversed(bits(size)):
            everything = jnp.concatenate([everything, swap(everything, axis, bit)], axis=0)
    spots = [0]
    for bit in reversed(bits(domains)):
        spots = spots + [i ^ bit for i in spots]
    spots = [i * groups for i in spots]
    for bit in reversed(bits(groups)):
        spots = spots + [i ^ bit for i in spots]

    lefts, self_term, upw, t1, s1, k1, t2, s2, k2, counts = left(
        groups, place, near_sources, near_counts, off, den, self_operator, upsample.T
    )
    far = far_field(groups, place, load, sort_loads(everything, spots, place, groups), rows)
    cols, tails = near(0, False, own, (t1, s1, k1), counts, cen, lefts, upw, ())
    out = near(
        1,
        True,
        sides[0] + sides[1],
        (t2, s2, k2),
        counts,
        cen,
        lefts,
        upw,
        (cols, tails, self_term, far),
    )
    return jnp.transpose(out, (1, 0, 2))


def sort_loads(held, spots, place, groups):
    position = [0] * len(spots)
    for i, spot in enumerate(spots):
        position[spot] = i
    table = jnp.asarray(position, jnp.int32)
    me = place[0] * groups + place[1]
    return held[table[jnp.arange(len(spots), dtype=jnp.int32) ^ me]]


def solution(mesh):
    in_specs = (
        P(("domain", "group"), None),
        P(("domain", "group"), None, None),
        P(("domain", "group"), None, None),
        P(("domain", "group"), None),
        P(),
        P(),
        P(("domain", "group"), None),
        P(("domain", "group")),
        P(("domain", "group")),
        P(("domain", "group"), None),
    )
    out_specs = P(("domain", "group"), None, None)
    return jax.shard_map(shards, mesh=mesh, in_specs=in_specs, out_specs=out_specs, check_vma=False)
```

```python
import functools

import jax
import jax.numpy as jnp
from jax import lax
from jax.experimental import pallas as pl
from jax.experimental.pallas import tpu as pltpu
from jax.sharding import PartitionSpec as P

LEAF_CAP = 16
EPS = 0.5
UNITS = 8
BATCH = 32
TAILS = 16
PADS = BATCH + 2 * UNITS
HALF = 48
F32 = jnp.float32
BF16 = jnp.bfloat16
HIGHEST = lax.Precision.HIGHEST
VMEM_SPEC = pl.BlockSpec(memory_space=pltpu.VMEM)
SMEM_SPEC = pl.BlockSpec(memory_space=pltpu.SMEM)


def params():
    return pltpu.CompilerParams(vmem_limit_bytes=60 << 20)


def cost(micros):
    return pl.CostEstimate(
        flops=int(micros * 1e9), bytes_accessed=int(micros * 3e6), transcendentals=0
    )


def iota(shape, dim):
    return lax.broadcasted_iota(jnp.int32, shape, dim)


def split3(value):
    high = value.astype(BF16).astype(F32)
    rest = value - high
    mid = rest.astype(BF16).astype(F32)
    return high, mid, rest - mid


def stack_left(value, axis):
    h, m, l = split3(value)
    return jnp.concatenate([h, m, l, h, m, h], axis=axis)


def stack_right(value, axis):
    h, m, l = split3(value)
    return jnp.concatenate([h, h, h, m, m, l], axis=axis)


def dot_nt(a, b, precision=None):
    return lax.dot_general(
        a, b, (((1,), (1,)), ((), ())), precision=precision, preferred_element_type=F32
    )


def column(row):
    n = row.shape[1]
    eye = iota((n, n), 0) == iota((n, n), 1)
    return jnp.sum(jnp.where(eye, row, jnp.zeros_like(row)), axis=1, keepdims=True)


def as_row(col):
    n = col.shape[0]
    eye = iota((n, n), 0) == iota((n, n), 1)
    return jnp.sum(jnp.where(eye, col, jnp.zeros_like(col)), axis=0, keepdims=True)


def pack_kernel(cen_ref, off_ref, den_ref, area_ref, leaf_ref, list_ref, tile_ref):
    rows, points = area_ref.shape
    area = area_ref[...]
    tail = points - 128
    tails = []
    lines = []
    for c in range(3):
        grid = off_ref[c] + column(cen_ref[c : c + 1, :])
        tile_ref[pl.ds(c, rows, 8), :] = grid[:, :128]
        tails.append(grid[:, 128:])
    tails.append(jnp.zeros((rows, tail), F32))
    for c in range(3):
        weighted = den_ref[c] * area
        tile_ref[pl.ds(4 + c, rows, 8), :] = weighted[:, :128]
        tails.append(weighted[:, 128:])
        lines.append(as_row(jnp.sum(weighted, axis=1, keepdims=True)))
    tails.append(jnp.zeros((rows, tail), F32))
    tile_ref[pl.ds(3, rows, 8), :] = jnp.concatenate(tails, axis=1)
    tile_ref[pl.ds(7, rows, 8), :] = jnp.zeros((rows, 128), F32)
    leaf = (leaf_ref[...] // LEAF_CAP).astype(F32)
    block = jnp.concatenate([cen_ref[...]] + lines + [leaf, jnp.zeros((1, rows), F32)], axis=0)
    lists = list_ref[...].astype(F32)
    rest = 128 - rows - lists.shape[1]
    tile_ref[8 * rows :, :] = jnp.concatenate([block, lists, jnp.zeros((8, rest), F32)], axis=1)


def pack(cen, off, den, area, leaf, lists):
    rows = area.shape[0]
    return pl.pallas_call(
        pack_kernel,
        out_shape=jax.ShapeDtypeStruct((8 * rows + 8, 128), F32),
        in_specs=[VMEM_SPEC] * 6,
        out_specs=VMEM_SPEC,
        compiler_params=params(),
        cost_estimate=cost(2),
        name="pack",
    )(cen, off, den, area, leaf, lists)


def quotient(value, by):
    if by & (by - 1) == 0:
        return lax.shift_right_logical(value, by.bit_length() - 1), jnp.bitwise_and(value, by - 1)
    return lax.div(value, by), lax.rem(value, by)


def encode(spot, slot, target):
    return spot * (1 << 12) + slot * (1 << 8) + target


def target_of(code):
    return jnp.bitwise_and(code, (1 << 8) - 1)


def slot_of(code):
    return jnp.bitwise_and(lax.shift_right_logical(code, 8), 15)


def spot_of(code):
    return lax.shift_right_logical(code, 12)


def list_kernel(groups, src_ref, cnt_ref, list_ref):
    slots, rows = src_ref.shape
    domain = lax.axis_index("domain")
    group = lax.axis_index("group")
    width = list_ref.shape[1]
    block = groups * rows

    def each_target(t, ends):
        live = cnt_ref[0, t]
        ends = list(ends)
        for k in range(slots):
            device, local = quotient(src_ref[k, t], rows)
            home, turn = quotient(device, groups)
            step = home - domain
            spot = jnp.bitwise_xor(turn, group) * rows + local + jnp.where(step > 0, block, 0)
            code = encode(spot, k, t)
            here = step == 0
            list_ref[jnp.where(here, 0, 1), jnp.where(here, ends[0], ends[1])] = code
            is_live = k < live
            ends[0] += jnp.where(jnp.logical_and(is_live, here), 1, 0)
            ends[1] += jnp.where(jnp.logical_and(is_live, jnp.logical_not(here)), 1, 0)
        return tuple(ends)

    ends = lax.fori_loop(0, rows, each_target, (0, 0))
    for which in range(2):
        list_ref[which, width - 1] = ends[which]

        def pad_one(i, _):
            list_ref[which, ends[which] + i] = encode((which + 1) * block, 0, 0)
            return 0

        lax.fori_loop(0, PADS, pad_one, 0)


def live_lists(groups, src, cnt):
    slots, rows = src.shape
    return pl.pallas_call(
        functools.partial(list_kernel, groups),
        out_shape=jax.ShapeDtypeStruct((2, rows * slots + PADS + 1), jnp.int32),
        in_specs=[SMEM_SPEC] * 2,
        out_specs=SMEM_SPEC,
        cost_estimate=cost(3),
        name="live_lists",
    )(src, cnt)


def setup_kernel(den_ref, op_ref, up_ref, self_ref, upw_ref):
    points = den_ref.shape[2]
    for c in range(3):
        self_ref[c] = dot_nt(den_ref[c], op_ref[...], HIGHEST)

    fine = up_ref.shape[1]
    full = fine // 128 * 128
    rest = fine - full
    tail = points - 128
    up = up_ref[...]
    wide = jnp.concatenate([up[:, :full]] + [up[:, full:]] * (128 // rest), axis=1)
    spare = jnp.zeros((128 - 6 * tail, full + 128), F32)
    upw_ref[...] = jnp.concatenate(
        [stack_right(wide[:128], 0), stack_right(wide[128:], 0), spare], axis=0
    ).astype(BF16)


def setup(den, op, up_t):
    fine = up_t.shape[1]
    return pl.pallas_call(
        setup_kernel,
        out_shape=(
            jax.ShapeDtypeStruct(den.shape, F32),
            jax.ShapeDtypeStruct((6 * 128 + 128, fine // 128 * 128 + 128), BF16),
        ),
        in_specs=[VMEM_SPEC] * 3,
        out_specs=(VMEM_SPEC,) * 2,
        compiler_params=params(),
        cost_estimate=cost(5),
        name="setup",
    )(den, op, up_t)


def left_kernel(off_ref, left_ref):
    _, rows, points = off_ref.shape
    eye = (iota((points, points), 0) == iota((points, points), 1)).astype(BF16)

    def one_left(t):
        x = [off_ref[c, pl.ds(t, 1), :] * (1.0 / EPS) for c in range(3)]
        xx = x[0] * x[0] + x[1] * x[1] + x[2] * x[2]
        one = jnp.ones_like(xx)
        zero = jnp.zeros_like(xx)
        cases = [x + [one, xx, zero, zero, zero]]
        for c in range(3):
            extra = [x[c] * x[b] for b in range(3)]
            extra[c] = extra[c] + xx
            cases.append(x + [one] + extra + [zero])
        stacked = [stack_left(jnp.concatenate(v, axis=0), 0) for v in cases]
        for p in range(2):
            both = jnp.concatenate(stacked[2 * p : 2 * p + 2], axis=0).astype(BF16)
            left_ref[t, p, :, : 2 * HALF] = dot_nt(eye, both).astype(BF16)

    each = 8

    def some_left(i, _):
        for j in range(each):
            one_left(i * each + j)
        return 0

    lax.fori_loop(0, rows // each, some_left, 0)


def left(off):
    _, rows, points = off.shape
    return pl.pallas_call(
        left_kernel,
        out_shape=jax.ShapeDtypeStruct((rows, 2, points, 128), BF16),
        in_specs=[VMEM_SPEC],
        out_specs=VMEM_SPEC,
        compiler_params=params(),
        cost_estimate=cost(10),
        name="left",
    )(off)


def right(ref):
    tile = ref[...]
    sub = iota(tile.shape, 0)
    y = [ref[c : c + 1, :] for c in range(3)]
    f = [ref[4 + c : 5 + c, :] for c in range(3)]
    yy = y[0] * y[0] + y[1] * y[1] + y[2] * y[2]
    yf = y[0] * f[0] + y[1] * f[1] + y[2] * f[2]
    rest = jnp.where(sub < 4, 0.0, tile)
    points = jnp.where(sub < 3, -2.0 * tile, jnp.where(sub == 3, yy + 2.0, 0.0))
    forces = jnp.where(sub < 3, -pltpu.roll(tile, 4, 0), jnp.where(sub == 3, yf, 0.0))
    outs = [points + jnp.where(sub == 3, -1.0, jnp.where(sub == 4, 1.0, 0.0))]
    for c in range(3):
        outs.append(f[c] * points + y[c] * forces + jnp.where(sub == c, -yf, rest))
    return [stack_right(v, 0).astype(BF16) for v in outs]


def shifted(tile, center):
    sub = iota(tile.shape, 0)
    shift = jnp.where(sub == 0, center[0], jnp.where(sub == 1, center[1], center[2]))
    return jnp.where(sub < 3, (tile - shift) * (1.0 / EPS), tile)


def place_right(w, parts):
    width = parts[0].shape[1]
    for o, part in enumerate(parts):
        h = o % 2
        w[o // 2, h * HALF : (h + 1) * HALF, h * width : (h + 1) * width] = part


def evaluate(lefts, w, width):
    sums = [0.0, 0.0, 0.0]
    total = w.shape[2] // 2
    for start in range(0, total, width):
        if width == total:
            wide = [
                jnp.dot(lefts[p], w[p], preferred_element_type=F32) for p in range(2)
            ]
            found = [v[:, h * width : (h + 1) * width] for v in wide for h in range(2)]
        else:
            found = [
                jnp.dot(
                    lefts[o // 2],
                    w[o // 2, :, o % 2 * total + start : o % 2 * total + start + width],
                    preferred_element_type=F32,
                )
                for o in range(4)
            ]
        u = lax.rsqrt(found[0])
        cube = u * u * u
        for c in range(3):
            product = cube * found[1 + c]
            for j in range(0, width, 128):
                sums[c] = sums[c] + product[:, j : j + 128]
    return [jnp.sum(s, axis=1, keepdims=True) for s in sums]


def near_kernel(n_blocks, which, last, groups, n_far, slots, *refs):
    list_ref, cen_ref = refs[:2]
    blocks = refs[2 : 2 + n_blocks]
    refs = refs[2 + n_blocks :]
    left_ref, upw_ref = refs[:2]
    refs = refs[2:]
    if last:
        cols_in, tail_in, self_ref = refs[:3]
        far_refs = refs[3 : 3 + n_far]
        out_ref = refs[3 + n_far]
        pool, fine, tails, cols, wa, wb, wt = refs[4 + n_far :]
    else:
        cols, tails, pool, fine, wa, wb = refs

    rows = left_ref.shape[0]
    points = left_ref.shape[2]
    full = upw_ref.shape[1] - 128
    for i, block in enumerate(blocks):
        pool[pl.ds(i * rows, rows)] = block[:rows]
    pool[n_blocks * rows] = jnp.zeros((8, 128), F32)
    wa[...] = jnp.zeros_like(wa)
    wb[...] = jnp.zeros_like(wb)
    if last:
        wt[...] = jnp.zeros_like(wt)
        cols[...] = cols_in[...]
        tails[...] = tail_in[...]
    else:
        cols[...] = jnp.zeros_like(cols)
        tails[...] = jnp.zeros_like(tails)

    n = list_ref[which, list_ref.shape[1] - 1]
    sub = iota((8, 128), 0)
    lane = iota((8, 128), 1)
    body = sub % 4 < 3
    tail = points - 128
    own_lanes = jnp.logical_and(lane // tail == sub, body)
    part = iota((8 * BATCH, 128), 1) // tail
    k_lane = lane // (128 // slots)

    def center_of(t):
        return [cen_ref[c, t] for c in range(3)]

    def upsample(b, _):
        tiles = [pool[spot_of(list_ref[which, b * BATCH + j])] for j in range(BATCH)]
        heads = jnp.concatenate([jnp.where(body, v, 0.0) for v in tiles], axis=0)
        ends = jnp.concatenate([jnp.where(own_lanes, v[3:4, :], 0.0) for v in tiles], axis=0)
        reach = tail
        while reach < 128:
            ends = ends + pltpu.roll(ends, reach, 1)
            reach *= 2
        h, m, l = split3(ends)
        ends = jnp.where(part == 2, l, jnp.where(jnp.logical_or(part == 1, part == 4), m, h))
        wide = jnp.concatenate([stack_left(heads, 1), ends], axis=1).astype(BF16)
        out = jnp.dot(wide, upw_ref[...], preferred_element_type=F32)
        out = out.reshape(BATCH, 8, full + 128)
        for j in range(BATCH):
            i = b * BATCH + j
            code = list_ref[which, i]
            t = target_of(code)
            center = center_of(t)
            fine[i] = shifted(out[j, :, :full], center)
            mine = jnp.logical_and(k_lane == slot_of(code), i < n)
            tails[t] = jnp.where(mine, shifted(out[j, :, full:], center), tails[t])
        return 0

    lax.fori_loop(0, (n + BATCH - 1) // BATCH, upsample, 0)

    lane_p = iota((points, 128), 1)

    def add_cols(found):
        for c in range(3):
            value = cols[c]
            for t, sums in found:
                value = value + jnp.where(lane_p == t, sums[c], 0.0)
            cols[c] = value

    def build(i, w):
        for j in range(UNITS):
            place_right(w.at[j], right(fine.at[i * UNITS + j]))

    def main(i, w):
        found = []
        for j in range(UNITS):
            t = target_of(list_ref[which, i * UNITS + j])
            lefts = [left_ref[t, p, :, : 2 * HALF] for p in range(2)]
            found.append((t, evaluate(lefts, w.at[j], 256)))
        add_cols(found)

    build(0, wa)

    def two(i, _):
        build(2 * i + 1, wb)
        main(2 * i, wa)
        build(2 * i + 2, wa)
        main(2 * i + 1, wb)
        return 0

    lax.fori_loop(0, (n + 2 * UNITS - 1) // (2 * UNITS), two, 0)

    if last:

        def tail_pass(i, _):
            found = []
            for j in range(TAILS):
                t = i * TAILS + j
                place_right(wt.at[j], right(tails.at[t]))
                lefts = [left_ref[t, p, :, : 2 * HALF] for p in range(2)]
                found.append((t, evaluate(lefts, wt.at[j], 128)))
            add_cols(found)
            return 0

        lax.fori_loop(0, rows // TAILS, tail_pass, 0)
        far = far_sums(groups, rows, far_refs)
        for c in range(3):
            turned = jnp.transpose(cols[c])[:rows]
            out_ref[c] = turned * (1.0 / EPS) + self_ref[c] + far[c]


def near(which, last, groups, blocks, lists, cen, lefts, upw, extra, far=()):
    rows, _, points, _ = lefts.shape
    full = upw.shape[1] - 128
    n_blocks = len(blocks)
    size = lists.shape[1] - 1
    slots = (size - PADS) // rows
    cols = jax.ShapeDtypeStruct((3, points, 128), F32)
    tails = jax.ShapeDtypeStruct((rows, 8, 128), F32)
    if last:
        out_shape = jax.ShapeDtypeStruct((3, rows, points), F32)
        out_specs = VMEM_SPEC
    else:
        out_shape = (cols, tails)
        out_specs = (VMEM_SPEC, VMEM_SPEC)
    scratch = [
        pltpu.VMEM((n_blocks * rows + 1, 8, 128), F32),
        pltpu.VMEM((size, 8, full), F32),
    ]
    if last:
        scratch += [pltpu.VMEM(tails.shape, F32), pltpu.VMEM(cols.shape, F32)]
    scratch += [pltpu.VMEM((UNITS, 2, 2 * HALF, 2 * full), BF16)] * 2
    if last:
        scratch += [pltpu.VMEM((TAILS, 2, 2 * HALF, 256), BF16)]
    n_vmem = n_blocks + 2 + len(extra) + len(far)
    return pl.pallas_call(
        functools.partial(near_kernel, n_blocks, which, last, groups, len(far), slots),
        out_shape=out_shape,
        in_specs=[SMEM_SPEC] * 2 + [VMEM_SPEC] * n_vmem,
        out_specs=out_specs,
        scratch_shapes=scratch,
        compiler_params=params(),
        cost_estimate=cost(25 if last else 15),
        name="near_last" if last else "near_own",
    )(lists, cen, *blocks, lefts, upw, *extra, *far)


def far_sums(groups, rows, refs):
    domain = lax.axis_index("domain")
    group = lax.axis_index("group")
    block = refs[0][0][:, :rows]
    center = [column(block[c : c + 1]) for c in range(3)]
    leaf = column(block[6:7])
    leaves = jnp.concatenate(
        [refs[0][jnp.bitwise_xor(group, g)][:, rows : rows + 8] for g in range(groups)], axis=0
    )
    count = groups * 8
    first = (domain * count).astype(F32)
    hot = (leaf - first == iota((rows, count), 1).astype(F32)).astype(F32)
    lists = jnp.dot(hot, leaves, precision=HIGHEST, preferred_element_type=F32)
    lists = jnp.round(lists)
    wanted = [jnp.broadcast_to(lists[:, k : k + 1], (rows, 128)) for k in range(8)]
    lane = iota((8, 128), 1)

    def one(ref, i, sums):
        both = jnp.where(lane < rows, ref[2 * i], pltpu.roll(ref[2 * i + 1], rows, 1))
        rel = [center[c] - both[c : c + 1] for c in range(3)]
        force = [both[3 + c : 4 + c] for c in range(3)]
        source = both[6:7]
        times = jnp.zeros((rows, 128), F32)
        for k in range(8):
            times = times + jnp.where(wanted[k] == source, 1.0, 0.0)
        dist = rel[0] * rel[0] + rel[1] * rel[1] + rel[2] * rel[2] + EPS * EPS
        u = lax.rsqrt(dist)
        u3 = u * u * u * times
        near_part = (dist + EPS * EPS) * u3
        project = (rel[0] * force[0] + rel[1] * force[1] + rel[2] * force[2]) * u3
        return [sums[c] + near_part * force[c] + project * rel[c] for c in range(3)]

    sums = [jnp.zeros((rows, 128), F32)] * 3
    for ref in refs:
        sums = lax.fori_loop(0, ref.shape[0] // 2, functools.partial(one, ref), sums)
    return [jnp.sum(v, axis=1, keepdims=True) for v in sums]


def swap(x, axis, bit):
    return lax.ppermute(x, axis, [(i, i ^ bit) for i in range(lax.axis_size(axis))])


def bits(n):
    found = []
    bit = 1
    while bit < n:
        found.append(bit)
        bit *= 2
    return found


def shards(
    centers,
    offsets,
    density,
    area,
    upsample,
    self_operator,
    near_sources,
    near_counts,
    leaf_slot,
    leaf_list,
):
    rows = centers.shape[0]
    groups = lax.axis_size("group")
    domains = lax.axis_size("domain")
    cen = centers.T
    off = jnp.transpose(offsets, (1, 0, 2))
    den = jnp.transpose(density, (1, 0, 2))
    tiles = pack(cen, off, den, area, leaf_slot[None, :], leaf_list)
    tiles = tiles.reshape(rows + 1, 8, 128)
    ends = domains - 1
    own = by_group(tiles, groups)
    above = lax.ppermute(tiles, "domain", [(i + 1, i) for i in range(ends)])
    below = lax.ppermute(tiles, "domain", [(i, i + 1) for i in range(ends)])

    lefts = left(off)
    own, src = after((own, near_sources), (lefts,))
    lists = live_lists(groups, src.T, near_counts[None, :])
    own, below, above, den = after((own, below, above, den), (lists,))
    sides = by_group(below, groups) + by_group(above, groups)
    steps = bits(domains)
    far = [jnp.concatenate([v[rows:] for v in own], axis=0)]
    far += combine(far, steps[:2])
    self_term, upw = setup(den, self_operator, upsample.T)
    far = after(far, (self_term,))
    for i in range(2, len(steps), 2):
        far += combine(far, steps[i : i + 2])
    lists = after(lists, far)
    cols, tails = near(0, False, groups, own, lists, cen, lefts, upw, ())
    out = near(
        1, True, groups, sides, lists, cen, lefts, upw, (cols, tails, self_term), far
    )
    return jnp.transpose(out, (1, 0, 2))


def after(values, others):
    return lax.optimization_barrier((values, others))[0]


def by_group(block, groups):
    return [block] + [swap(block, "group", i) for i in range(1, groups)]


def combine(held, steps):
    whole = held[0] if len(held) == 1 else jnp.concatenate(held, axis=0)
    masks = [steps[0]] if len(steps) == 1 else [steps[0], steps[1], steps[0] ^ steps[1]]
    return [swap(whole, "domain", mask) for mask in masks]


def solution(mesh):
    in_specs = (
        P(("domain", "group"), None),
        P(("domain", "group"), None, None),
        P(("domain", "group"), None, None),
        P(("domain", "group"), None),
        P(),
        P(),
        P(("domain", "group"), None),
        P(("domain", "group")),
        P(("domain", "group")),
        P(("domain", "group"), None),
    )
    out_specs = P(("domain", "group"), None, None)
    return jax.shard_map(shards, mesh=mesh, in_specs=in_specs, out_specs=out_specs, check_vma=False)
```

```python
import functools

import jax
import jax.numpy as jnp
from jax import lax
from jax.experimental import pallas as pl
from jax.experimental.pallas import tpu as pltpu
from jax.sharding import PartitionSpec as P

LEAF_CAP = 16
EPS = 0.5
UNITS = 8
BATCH = 32
TAILS = 16
PADS = BATCH + 2 * UNITS
HALF = 48
F32 = jnp.float32
BF16 = jnp.bfloat16
HIGHEST = lax.Precision.HIGHEST
VMEM_SPEC = pl.BlockSpec(memory_space=pltpu.VMEM)
SMEM_SPEC = pl.BlockSpec(memory_space=pltpu.SMEM)


def params(mib=60):
    return pltpu.CompilerParams(vmem_limit_bytes=mib << 20)


def cost(micros):
    return pl.CostEstimate(
        flops=int(micros * 1e9), bytes_accessed=int(micros * 3e6), transcendentals=0
    )


def iota(shape, dim):
    return lax.broadcasted_iota(jnp.int32, shape, dim)


def split3(value):
    high = value.astype(BF16).astype(F32)
    rest = value - high
    mid = rest.astype(BF16).astype(F32)
    return high, mid, rest - mid


def stack_left(value, axis):
    h, m, l = split3(value)
    return jnp.concatenate([h, m, l, h, m, h], axis=axis)


def stack_right(value, axis):
    h, m, l = split3(value)
    return jnp.concatenate([h, h, h, m, m, l], axis=axis)


def dot_nt(a, b, precision=None):
    return lax.dot_general(
        a, b, (((1,), (1,)), ((), ())), precision=precision, preferred_element_type=F32
    )


def column(row):
    n = row.shape[1]
    eye = iota((n, n), 0) == iota((n, n), 1)
    return jnp.sum(jnp.where(eye, row, jnp.zeros_like(row)), axis=1, keepdims=True)


def as_row(col):
    n = col.shape[0]
    eye = iota((n, n), 0) == iota((n, n), 1)
    return jnp.sum(jnp.where(eye, col, jnp.zeros_like(col)), axis=0, keepdims=True)


def pack_kernel(cen_ref, off_ref, den_ref, area_ref, leaf_ref, list_ref, tile_ref):
    rows, points = area_ref.shape
    area = area_ref[...]
    tail = points - 128
    tails = []
    lines = []
    for c in range(3):
        grid = off_ref[c] + column(cen_ref[c : c + 1, :])
        tile_ref[pl.ds(c, rows, 8), :] = grid[:, :128]
        tails.append(grid[:, 128:])
    tails.append(jnp.zeros((rows, tail), F32))
    for c in range(3):
        weighted = den_ref[c] * area
        tile_ref[pl.ds(4 + c, rows, 8), :] = weighted[:, :128]
        tails.append(weighted[:, 128:])
        lines.append(as_row(jnp.sum(weighted, axis=1, keepdims=True)))
    tails.append(jnp.zeros((rows, tail), F32))
    tile_ref[pl.ds(3, rows, 8), :] = jnp.concatenate(tails, axis=1)
    tile_ref[pl.ds(7, rows, 8), :] = jnp.zeros((rows, 128), F32)
    leaf = (leaf_ref[...] // LEAF_CAP).astype(F32)
    block = jnp.concatenate([cen_ref[...]] + lines + [leaf, jnp.zeros((1, rows), F32)], axis=0)
    lists = list_ref[...].astype(F32)
    rest = 128 - rows - lists.shape[1]
    tile_ref[8 * rows :, :] = jnp.concatenate([block, lists, jnp.zeros((8, rest), F32)], axis=1)


def pack(cen, off, den, area, leaf, lists):
    rows = area.shape[0]
    return pl.pallas_call(
        pack_kernel,
        out_shape=jax.ShapeDtypeStruct((8 * rows + 8, 128), F32),
        in_specs=[VMEM_SPEC] * 6,
        out_specs=VMEM_SPEC,
        compiler_params=params(),
        cost_estimate=cost(2),
        name="pack",
    )(cen, off, den, area, leaf, lists)


def quotient(value, by):
    if by & (by - 1) == 0:
        return lax.shift_right_logical(value, by.bit_length() - 1), jnp.bitwise_and(value, by - 1)
    return lax.div(value, by), lax.rem(value, by)


def encode(spot, slot, target):
    return spot * (1 << 12) + slot * (1 << 8) + target


def target_of(code):
    return jnp.bitwise_and(code, (1 << 8) - 1)


def slot_of(code):
    return jnp.bitwise_and(lax.shift_right_logical(code, 8), 15)


def spot_of(code):
    return lax.shift_right_logical(code, 12)


def add_pairs(groups, src_ref, cnt_ref, list_ref, t, ends):
    slots, rows = src_ref.shape
    domain = lax.axis_index("domain")
    group = lax.axis_index("group")
    live = cnt_ref[0, t]
    ends = list(ends)
    for k in range(slots):
        device, local = quotient(src_ref[k, t], rows)
        home, turn = quotient(device, groups)
        step = home - domain
        here = step == 0
        held = jnp.where(here, rows, 2 * rows)
        spot = jnp.bitwise_xor(turn, group) * held + local + jnp.where(step > 0, rows, 0)
        list_ref[jnp.where(here, 0, 1), jnp.where(here, ends[0], ends[1])] = encode(spot, k, t)
        is_live = k < live
        ends[0] += jnp.where(jnp.logical_and(is_live, here), 1, 0)
        ends[1] += jnp.where(jnp.logical_and(is_live, jnp.logical_not(here)), 1, 0)
    return tuple(ends)


def end_lists(block, list_ref, ends):
    width = list_ref.shape[1]
    for which in range(2):
        list_ref[which, width - 1] = ends[which]
        for i in range(PADS):
            list_ref[which, ends[which] + i] = encode((which + 1) * block, 0, 0)


def setup_kernel(den_ref, op_ref, up_ref, self_ref, upw_ref):
    points = den_ref.shape[2]
    for c in range(3):
        self_ref[c] = dot_nt(den_ref[c], op_ref[...], HIGHEST)

    fine = up_ref.shape[1]
    full = fine // 128 * 128
    rest = fine - full
    tail = points - 128
    up = up_ref[...]
    wide = jnp.concatenate([up[:, :full]] + [up[:, full:]] * (128 // rest), axis=1)
    spare = jnp.zeros((128 - 6 * tail, full + 128), F32)
    upw_ref[...] = jnp.concatenate(
        [stack_right(wide[:128], 0), stack_right(wide[128:], 0), spare], axis=0
    ).astype(BF16)


def setup(den, op, up_t):
    fine = up_t.shape[1]
    return pl.pallas_call(
        setup_kernel,
        out_shape=(
            jax.ShapeDtypeStruct(den.shape, F32),
            jax.ShapeDtypeStruct((6 * 128 + 128, fine // 128 * 128 + 128), BF16),
        ),
        in_specs=[VMEM_SPEC] * 3,
        out_specs=(VMEM_SPEC,) * 2,
        compiler_params=params(24),
        cost_estimate=cost(5),
        name="setup",
    )(den, op, up_t)


def left_kernel(groups, src_ref, cnt_ref, off_ref, left_ref, list_ref):
    _, rows, points = off_ref.shape
    eye = (iota((points, points), 0) == iota((points, points), 1)).astype(BF16)

    def one_left(t):
        x = [off_ref[c, pl.ds(t, 1), :] * (1.0 / EPS) for c in range(3)]
        xx = x[0] * x[0] + x[1] * x[1] + x[2] * x[2]
        one = jnp.ones_like(xx)
        zero = jnp.zeros_like(xx)
        cases = [x + [one, xx, zero, zero, zero]]
        for c in range(3):
            extra = [x[c] * x[b] for b in range(3)]
            extra[c] = extra[c] + xx
            cases.append(x + [one] + extra + [zero])
        stacked = [stack_left(jnp.concatenate(v, axis=0), 0) for v in cases]
        for p in range(2):
            both = jnp.concatenate(stacked[2 * p : 2 * p + 2], axis=0).astype(BF16)
            left_ref[t, p, :, : 2 * HALF] = dot_nt(eye, both).astype(BF16)

    each = 8

    def some_left(i, ends):
        for j in range(each):
            ends = add_pairs(groups, src_ref, cnt_ref, list_ref, i * each + j, ends)
            one_left(i * each + j)
        return ends

    ends = lax.fori_loop(0, rows // each, some_left, (0, 0))
    end_lists(groups * rows, list_ref, ends)


def left(groups, src, cnt, off):
    _, rows, points = off.shape
    return pl.pallas_call(
        functools.partial(left_kernel, groups),
        out_shape=(
            jax.ShapeDtypeStruct((rows, 2, points, 128), BF16),
            jax.ShapeDtypeStruct((2, src.shape[0] * rows + PADS + 1), jnp.int32),
        ),
        in_specs=[SMEM_SPEC] * 2 + [VMEM_SPEC],
        out_specs=(VMEM_SPEC, SMEM_SPEC),
        compiler_params=params(24),
        cost_estimate=cost(10),
        name="left",
    )(src, cnt, off)


def right(ref):
    tile = ref[...]
    sub = iota(tile.shape, 0)
    y = [ref[c : c + 1, :] for c in range(3)]
    f = [ref[4 + c : 5 + c, :] for c in range(3)]
    yy = y[0] * y[0] + y[1] * y[1] + y[2] * y[2]
    yf = y[0] * f[0] + y[1] * f[1] + y[2] * f[2]
    rest = jnp.where(sub < 4, 0.0, tile)
    points = jnp.where(sub < 3, -2.0 * tile, jnp.where(sub == 3, yy + 2.0, 0.0))
    forces = jnp.where(sub < 3, -pltpu.roll(tile, 4, 0), jnp.where(sub == 3, yf, 0.0))
    outs = [points + jnp.where(sub == 3, -1.0, jnp.where(sub == 4, 1.0, 0.0))]
    for c in range(3):
        outs.append(f[c] * points + y[c] * forces + jnp.where(sub == c, -yf, rest))
    return [stack_right(v, 0).astype(BF16) for v in outs]


def shifted(tile, center):
    sub = iota(tile.shape, 0)
    shift = jnp.where(sub == 0, center[0], jnp.where(sub == 1, center[1], center[2]))
    return jnp.where(sub < 3, (tile - shift) * (1.0 / EPS), tile)


def place_right(w, parts):
    width = parts[0].shape[1]
    for o, part in enumerate(parts):
        h = o % 2
        w[o // 2, h * HALF : (h + 1) * HALF, h * width : (h + 1) * width] = part


def evaluate(lefts, w, width):
    sums = [0.0, 0.0, 0.0]
    total = w.shape[2] // 2
    for start in range(0, total, width):
        if width == total:
            wide = [
                jnp.dot(lefts[p], w[p], preferred_element_type=F32) for p in range(2)
            ]
            found = [v[:, h * width : (h + 1) * width] for v in wide for h in range(2)]
        else:
            found = [
                jnp.dot(
                    lefts[o // 2],
                    w[o // 2, :, o % 2 * total + start : o % 2 * total + start + width],
                    preferred_element_type=F32,
                )
                for o in range(4)
            ]
        u = lax.rsqrt(found[0])
        cube = u * u * u
        for c in range(3):
            product = cube * found[1 + c]
            for j in range(0, width, 128):
                sums[c] = sums[c] + product[:, j : j + 128]
    return [jnp.sum(s, axis=1, keepdims=True) for s in sums]


def near_kernel(n_blocks, which, last, groups, n_far, slots, *refs):
    list_ref, cen_ref = refs[:2]
    blocks = refs[2 : 2 + n_blocks]
    refs = refs[2 + n_blocks :]
    left_ref, upw_ref = refs[:2]
    refs = refs[2:]
    if last:
        cols_in, tail_in, self_ref = refs[:3]
        far_refs = refs[3 : 3 + n_far]
        out_ref = refs[3 + n_far]
        pool, fine, tails, cols, wa, wb, wt = refs[4 + n_far :]
    else:
        cols, tails, pool, fine, wa, wb = refs

    rows = left_ref.shape[0]
    points = left_ref.shape[2]
    full = upw_ref.shape[1] - 128
    held = blocks[0].shape[0] // rows * rows
    for i, block in enumerate(blocks):
        pool[pl.ds(i * held, held)] = block[:held]
    pool[n_blocks * held] = jnp.zeros((8, 128), F32)
    wa[...] = jnp.zeros_like(wa)
    wb[...] = jnp.zeros_like(wb)
    if last:
        wt[...] = jnp.zeros_like(wt)
        cols[...] = cols_in[...]
        tails[...] = tail_in[...]
    else:
        cols[...] = jnp.zeros_like(cols)
        tails[...] = jnp.zeros_like(tails)

    n = list_ref[which, list_ref.shape[1] - 1]
    sub = iota((8, 128), 0)
    lane = iota((8, 128), 1)
    body = sub % 4 < 3
    tail = points - 128
    own_lanes = jnp.logical_and(lane // tail == sub, body)
    part = iota((8 * BATCH, 128), 1) // tail
    k_lane = lane // (128 // slots)

    def center_of(t):
        return [cen_ref[c, t] for c in range(3)]

    def upsample(b, _):
        tiles = [pool[spot_of(list_ref[which, b * BATCH + j])] for j in range(BATCH)]
        heads = jnp.concatenate([jnp.where(body, v, 0.0) for v in tiles], axis=0)
        ends = jnp.concatenate([jnp.where(own_lanes, v[3:4, :], 0.0) for v in tiles], axis=0)
        reach = tail
        while reach < 128:
            ends = ends + pltpu.roll(ends, reach, 1)
            reach *= 2
        h, m, l = split3(ends)
        ends = jnp.where(part == 2, l, jnp.where(jnp.logical_or(part == 1, part == 4), m, h))
        wide = jnp.concatenate([stack_left(heads, 1), ends], axis=1).astype(BF16)
        out = jnp.dot(wide, upw_ref[...], preferred_element_type=F32)
        out = out.reshape(BATCH, 8, full + 128)
        for j in range(BATCH):
            i = b * BATCH + j
            code = list_ref[which, i]
            t = target_of(code)
            center = center_of(t)
            fine[i] = shifted(out[j, :, :full], center)
            mine = jnp.logical_and(k_lane == slot_of(code), i < n)
            tails[t] = jnp.where(mine, shifted(out[j, :, full:], center), tails[t])
        return 0

    lax.fori_loop(0, (n + BATCH - 1) // BATCH, upsample, 0)

    lane_p = iota((points, 128), 1)

    def add_cols(found):
        for c in range(3):
            value = cols[c]
            for t, sums in found:
                value = value + jnp.where(lane_p == t, sums[c], 0.0)
            cols[c] = value

    def build(i, w):
        for j in range(UNITS):
            place_right(w.at[j], right(fine.at[i * UNITS + j]))

    def main(i, w):
        found = []
        for j in range(UNITS):
            t = target_of(list_ref[which, i * UNITS + j])
            lefts = [left_ref[t, p, :, : 2 * HALF] for p in range(2)]
            found.append((t, evaluate(lefts, w.at[j], 256)))
        add_cols(found)

    build(0, wa)

    def two(i, _):
        build(2 * i + 1, wb)
        main(2 * i, wa)
        build(2 * i + 2, wa)
        main(2 * i + 1, wb)
        return 0

    lax.fori_loop(0, (n + 2 * UNITS - 1) // (2 * UNITS), two, 0)

    if last:

        def tail_pass(i, _):
            found = []
            for j in range(TAILS):
                t = i * TAILS + j
                place_right(wt.at[j], right(tails.at[t]))
                lefts = [left_ref[t, p, :, : 2 * HALF] for p in range(2)]
                found.append((t, evaluate(lefts, wt.at[j], 128)))
            for c in range(3):
                value = jnp.zeros((points, 128), F32)
                for t, sums in found:
                    value = jnp.where(lane_p == t, sums[c], value)
                cols[c] += value
            return 0

        lax.fori_loop(0, rows // TAILS, tail_pass, 0)
        far = far_sums(groups, rows, far_refs)
        for c in range(3):
            turned = jnp.transpose(cols[c])[:rows]
            out_ref[c] = turned * (1.0 / EPS) + self_ref[c] + far[c]


def near(which, last, groups, blocks, lists, cen, lefts, upw, extra, far=()):
    rows, _, points, _ = lefts.shape
    full = upw.shape[1] - 128
    n_blocks = len(blocks)
    size = lists.shape[1] - 1
    slots = (size - PADS) // rows
    cols = jax.ShapeDtypeStruct((3, points, 128), F32)
    tails = jax.ShapeDtypeStruct((rows, 8, 128), F32)
    if last:
        out_shape = jax.ShapeDtypeStruct((3, rows, points), F32)
        out_specs = VMEM_SPEC
    else:
        out_shape = (cols, tails)
        out_specs = (VMEM_SPEC, VMEM_SPEC)
    scratch = [
        pltpu.VMEM((n_blocks * (blocks[0].shape[0] // rows * rows) + 1, 8, 128), F32),
        pltpu.VMEM((size, 8, full), F32),
    ]
    if last:
        scratch += [pltpu.VMEM(tails.shape, F32), pltpu.VMEM(cols.shape, F32)]
    scratch += [pltpu.VMEM((UNITS, 2, 2 * HALF, 2 * full), BF16)] * 2
    if last:
        scratch += [pltpu.VMEM((TAILS, 2, 2 * HALF, 256), BF16)]
    n_vmem = n_blocks + 2 + len(extra) + len(far)
    return pl.pallas_call(
        functools.partial(near_kernel, n_blocks, which, last, groups, len(far), slots),
        out_shape=out_shape,
        in_specs=[SMEM_SPEC] * 2 + [VMEM_SPEC] * n_vmem,
        out_specs=out_specs,
        scratch_shapes=scratch,
        compiler_params=params(44),
        cost_estimate=cost(25 if last else 0.3),
        name="near_last" if last else "near_own",
    )(lists, cen, *blocks, lefts, upw, *extra, *far)


def far_sums(groups, rows, refs):
    domain = lax.axis_index("domain")
    group = lax.axis_index("group")
    block = refs[0][0][:, :rows]
    center = [column(block[c : c + 1]) for c in range(3)]
    leaf = column(block[6:7])
    leaves = jnp.concatenate(
        [refs[0][jnp.bitwise_xor(group, g)][:, rows : rows + 8] for g in range(groups)], axis=0
    )
    count = groups * 8
    first = (domain * count).astype(F32)
    hot = (leaf - first == iota((rows, count), 1).astype(F32)).astype(F32)
    lists = jnp.dot(hot, leaves, precision=HIGHEST, preferred_element_type=F32)
    lists = jnp.round(lists)
    wanted = [jnp.broadcast_to(lists[:, k : k + 1], (rows, 128)) for k in range(8)]
    lane = iota((8, 128), 1)

    def one(ref, i, sums):
        both = jnp.where(lane < rows, ref[2 * i], pltpu.roll(ref[2 * i + 1], rows, 1))
        rel = [center[c] - both[c : c + 1] for c in range(3)]
        force = [both[3 + c : 4 + c] for c in range(3)]
        source = both[6:7]
        times = jnp.zeros((rows, 128), F32)
        for k in range(8):
            times = times + jnp.where(wanted[k] == source, 1.0, 0.0)
        dist = rel[0] * rel[0] + rel[1] * rel[1] + rel[2] * rel[2] + EPS * EPS
        u = lax.rsqrt(dist)
        u3 = u * u * u * times
        near_part = (dist + EPS * EPS) * u3
        project = (rel[0] * force[0] + rel[1] * force[1] + rel[2] * force[2]) * u3
        return [sums[c] + near_part * force[c] + project * rel[c] for c in range(3)]

    sums = [jnp.zeros((rows, 128), F32)] * 3
    for ref in refs:
        sums = lax.fori_loop(0, ref.shape[0] // 2, functools.partial(one, ref), sums, unroll=min(4, ref.shape[0] // 2))
    return [jnp.sum(v, axis=1, keepdims=True) for v in sums]


def swap(x, axis, bit):
    return lax.ppermute(x, axis, [(i, i ^ bit) for i in range(lax.axis_size(axis))])


def bits(n):
    found = []
    bit = 1
    while bit < n:
        found.append(bit)
        bit *= 2
    return found


def shards(
    centers,
    offsets,
    density,
    area,
    upsample,
    self_operator,
    near_sources,
    near_counts,
    leaf_slot,
    leaf_list,
):
    rows = centers.shape[0]
    groups = lax.axis_size("group")
    domains = lax.axis_size("domain")
    cen = centers.T
    off = jnp.transpose(offsets, (1, 0, 2))
    den = jnp.transpose(density, (1, 0, 2))
    tiles = pack(cen, off, den, area, leaf_slot[None, :], leaf_list)
    tiles = tiles.reshape(rows + 1, 8, 128)
    ends = domains - 1
    above = lax.ppermute(tiles, "domain", [(i + 1, i) for i in range(ends)])
    below = lax.ppermute(tiles, "domain", [(i, i + 1) for i in range(ends)])
    own = by_group(tiles, groups)

    lefts, lists = left(groups, near_sources.T, near_counts[None, :], off)
    own, below, above, den = after((own, below, above, den), (lefts,))
    both = jnp.concatenate([below[:rows], above[:rows]], axis=0)
    far = [jnp.concatenate([v[rows:] for v in own], axis=0)]
    hops = []
    steps = bits(domains)
    self_term = None
    for turn in range(max(len(steps), groups - 1)):
        if turn < len(steps):
            far.append(swap(jnp.concatenate(far, axis=0), "domain", steps[turn]))
        if turn + 1 < groups:
            hops.append(swap(both, "group", turn + 1))
        if turn == 0:
            self_term, upw = setup(den, self_operator, upsample.T)
            far = after(far, (self_term,))
    sides = [both] + hops
    lists = after(lists, far[:-1])
    cols, tails = near(0, False, groups, own, lists, cen, lefts, upw, ())
    out = near(
        1, True, groups, sides, lists, cen, lefts, upw, (cols, tails, self_term), far
    )
    return jnp.transpose(out, (1, 0, 2))


def after(values, others):
    return lax.optimization_barrier((values, others))[0]


def by_group(block, groups):
    return [block] + [swap(block, "group", i) for i in range(1, groups)]


def combine(held, steps):
    whole = held[0] if len(held) == 1 else jnp.concatenate(held, axis=0)
    masks = [steps[0]] if len(steps) == 1 else [steps[0], steps[1], steps[0] ^ steps[1]]
    return [swap(whole, "domain", mask) for mask in masks]


def solution(mesh):
    in_specs = (
        P(("domain", "group"), None),
        P(("domain", "group"), None, None),
        P(("domain", "group"), None, None),
        P(("domain", "group"), None),
        P(),
        P(),
        P(("domain", "group"), None),
        P(("domain", "group")),
        P(("domain", "group")),
        P(("domain", "group"), None),
    )
    out_specs = P(("domain", "group"), None, None)
    return jax.shard_map(shards, mesh=mesh, in_specs=in_specs, out_specs=out_specs, check_vma=False)
```

```python
import functools

import jax
import jax.numpy as jnp
from jax import lax
from jax.experimental import pallas as pl
from jax.experimental.pallas import tpu as pltpu
from jax.sharding import PartitionSpec as P

LEAF_CAP = 16
EPS = 0.5
UNITS = 8
BATCH = 32
TAILS = 16
LINES = 7
PADS = BATCH + 2 * UNITS
HALF = 48
F32 = jnp.float32
BF16 = jnp.bfloat16
HIGHEST = lax.Precision.HIGHEST
VMEM_SPEC = pl.BlockSpec(memory_space=pltpu.VMEM)
SMEM_SPEC = pl.BlockSpec(memory_space=pltpu.SMEM)


def params(mib=60):
    return pltpu.CompilerParams(vmem_limit_bytes=mib << 20)


def cost(micros):
    return pl.CostEstimate(
        flops=int(micros * 1e9), bytes_accessed=int(micros * 3e6), transcendentals=0
    )


def iota(shape, dim):
    return lax.broadcasted_iota(jnp.int32, shape, dim)


def split3(value):
    high = value.astype(BF16).astype(F32)
    rest = value - high
    mid = rest.astype(BF16).astype(F32)
    return high, mid, rest - mid


def stack_left(value, axis):
    h, m, l = split3(value)
    return jnp.concatenate([h, m, l, h, m, h], axis=axis)


def stack_right(value, axis):
    h, m, l = split3(value)
    return jnp.concatenate([h, h, h, m, m, l], axis=axis)


def dot_nt(a, b, precision=None):
    return lax.dot_general(
        a, b, (((1,), (1,)), ((), ())), precision=precision, preferred_element_type=F32
    )


def column(row):
    n = row.shape[1]
    eye = iota((n, n), 0) == iota((n, n), 1)
    return jnp.sum(jnp.where(eye, row, jnp.zeros_like(row)), axis=1, keepdims=True)


def as_row(col):
    n = col.shape[0]
    eye = iota((n, n), 0) == iota((n, n), 1)
    return jnp.sum(jnp.where(eye, col, jnp.zeros_like(col)), axis=0, keepdims=True)


def pack_kernel(cen_ref, off_ref, den_ref, area_ref, leaf_ref, list_ref, tile_ref):
    rows, points = area_ref.shape
    area = area_ref[...]
    tail = points - 128
    tails = []
    lines = []
    for c in range(3):
        grid = off_ref[c] + column(cen_ref[c : c + 1, :])
        tile_ref[pl.ds(c, rows, LINES), :] = grid[:, :128]
        tails.append(grid[:, 128:])
    tails.append(jnp.zeros((rows, tail), F32))
    for c in range(3):
        weighted = den_ref[c] * area
        tile_ref[pl.ds(4 + c, rows, LINES), :] = weighted[:, :128]
        tails.append(weighted[:, 128:])
        lines.append(as_row(jnp.sum(weighted, axis=1, keepdims=True)))
    tails.append(jnp.zeros((rows, tail), F32))
    tile_ref[pl.ds(3, rows, LINES), :] = jnp.concatenate(tails, axis=1)
    leaf = (leaf_ref[...] // LEAF_CAP).astype(F32)
    block = jnp.concatenate([cen_ref[...]] + lines + [leaf, jnp.zeros((1, rows), F32)], axis=0)
    lists = list_ref[...].astype(F32)
    rest = 128 - rows - lists.shape[1]
    tile_ref[LINES * rows :, :] = jnp.concatenate([block, lists, jnp.zeros((8, rest), F32)], axis=1)


def pack(cen, off, den, area, leaf, lists):
    rows = area.shape[0]
    return pl.pallas_call(
        pack_kernel,
        out_shape=jax.ShapeDtypeStruct((LINES * rows + 8, 128), F32),
        in_specs=[VMEM_SPEC] * 6,
        out_specs=VMEM_SPEC,
        compiler_params=params(),
        cost_estimate=cost(2),
        name="pack",
    )(cen, off, den, area, leaf, lists)


def quotient(value, by):
    if by & (by - 1) == 0:
        return lax.shift_right_logical(value, by.bit_length() - 1), jnp.bitwise_and(value, by - 1)
    return lax.div(value, by), lax.rem(value, by)


def encode(spot, slot, target):
    return spot * (1 << 12) + slot * (1 << 8) + target


def target_of(code):
    return jnp.bitwise_and(code, (1 << 8) - 1)


def slot_of(code):
    return jnp.bitwise_and(lax.shift_right_logical(code, 8), 15)


def spot_of(code):
    return lax.shift_right_logical(code, 12)


def add_pairs(groups, src_ref, cnt_ref, list_ref, t, ends):
    slots, rows = src_ref.shape
    domain = lax.axis_index("domain")
    group = lax.axis_index("group")
    live = cnt_ref[0, t]
    ends = list(ends)
    for k in range(slots):
        device, local = quotient(src_ref[k, t], rows)
        home, turn = quotient(device, groups)
        step = home - domain
        here = step == 0
        held = jnp.where(here, rows, 2 * rows)
        spot = jnp.bitwise_xor(turn, group) * held + local + jnp.where(step > 0, rows, 0)
        list_ref[jnp.where(here, 0, 1), jnp.where(here, ends[0], ends[1])] = encode(spot, k, t)
        is_live = k < live
        ends[0] += jnp.where(jnp.logical_and(is_live, here), 1, 0)
        ends[1] += jnp.where(jnp.logical_and(is_live, jnp.logical_not(here)), 1, 0)
    return tuple(ends)


def end_lists(block, list_ref, ends):
    width = list_ref.shape[1]
    for which in range(2):
        list_ref[which, width - 1] = ends[which]
        for i in range(PADS):
            list_ref[which, ends[which] + i] = encode((which + 1) * block, 0, 0)


def setup_kernel(den_ref, op_ref, up_ref, self_ref, upw_ref):
    points = den_ref.shape[2]
    for c in range(3):
        self_ref[c] = dot_nt(den_ref[c], op_ref[...], HIGHEST)

    fine = up_ref.shape[1]
    full = fine // 128 * 128
    rest = fine - full
    tail = points - 128
    up = up_ref[...]
    wide = jnp.concatenate([up[:, :full]] + [up[:, full:]] * (128 // rest), axis=1)
    spare = jnp.zeros((128 - 6 * tail, full + 128), F32)
    upw_ref[...] = jnp.concatenate(
        [stack_right(wide[:128], 0), stack_right(wide[128:], 0), spare], axis=0
    ).astype(BF16)


def setup(den, op, up_t):
    fine = up_t.shape[1]
    return pl.pallas_call(
        setup_kernel,
        out_shape=(
            jax.ShapeDtypeStruct(den.shape, F32),
            jax.ShapeDtypeStruct((6 * 128 + 128, fine // 128 * 128 + 128), BF16),
        ),
        in_specs=[VMEM_SPEC] * 3,
        out_specs=(VMEM_SPEC,) * 2,
        compiler_params=params(24),
        cost_estimate=cost(5),
        name="setup",
    )(den, op, up_t)


def left_kernel(groups, src_ref, cnt_ref, off_ref, left_ref, list_ref):
    _, rows, points = off_ref.shape
    eye = (iota((points, points), 0) == iota((points, points), 1)).astype(BF16)

    def one_left(t):
        x = [off_ref[c, pl.ds(t, 1), :] * (1.0 / EPS) for c in range(3)]
        xx = x[0] * x[0] + x[1] * x[1] + x[2] * x[2]
        one = jnp.ones_like(xx)
        zero = jnp.zeros_like(xx)
        cases = [x + [one, xx, zero, zero, zero]]
        for c in range(3):
            extra = [x[c] * x[b] for b in range(3)]
            extra[c] = extra[c] + xx
            cases.append(x + [one] + extra + [zero])
        stacked = [stack_left(jnp.concatenate(v, axis=0), 0) for v in cases]
        for p in range(2):
            both = jnp.concatenate(stacked[2 * p : 2 * p + 2], axis=0).astype(BF16)
            left_ref[t, p, :, : 2 * HALF] = dot_nt(eye, both).astype(BF16)

    each = 8

    def some_left(i, ends):
        for j in range(each):
            ends = add_pairs(groups, src_ref, cnt_ref, list_ref, i * each + j, ends)
            one_left(i * each + j)
        return ends

    ends = lax.fori_loop(0, rows // each, some_left, (0, 0))
    end_lists(groups * rows, list_ref, ends)


def left(groups, src, cnt, off):
    _, rows, points = off.shape
    return pl.pallas_call(
        functools.partial(left_kernel, groups),
        out_shape=(
            jax.ShapeDtypeStruct((rows, 2, points, 128), BF16),
            jax.ShapeDtypeStruct((2, src.shape[0] * rows + PADS + 1), jnp.int32),
        ),
        in_specs=[SMEM_SPEC] * 2 + [VMEM_SPEC],
        out_specs=(VMEM_SPEC, SMEM_SPEC),
        compiler_params=params(24),
        cost_estimate=cost(10),
        name="left",
    )(src, cnt, off)


def right(ref):
    tile = ref[...]
    sub = iota(tile.shape, 0)
    y = [ref[c : c + 1, :] for c in range(3)]
    f = [ref[4 + c : 5 + c, :] for c in range(3)]
    yy = y[0] * y[0] + y[1] * y[1] + y[2] * y[2]
    yf = y[0] * f[0] + y[1] * f[1] + y[2] * f[2]
    rest = jnp.where(sub < 4, 0.0, tile)
    points = jnp.where(sub < 3, -2.0 * tile, jnp.where(sub == 3, yy + 2.0, 0.0))
    forces = jnp.where(sub < 3, -pltpu.roll(tile, 4, 0), jnp.where(sub == 3, yf, 0.0))
    outs = [points + jnp.where(sub == 3, -1.0, jnp.where(sub == 4, 1.0, 0.0))]
    for c in range(3):
        outs.append(f[c] * points + y[c] * forces + jnp.where(sub == c, -yf, rest))
    return [stack_right(v, 0).astype(BF16) for v in outs]


def shifted(tile, center):
    sub = iota(tile.shape, 0)
    shift = jnp.where(sub == 0, center[0], jnp.where(sub == 1, center[1], center[2]))
    return jnp.where(sub < 3, (tile - shift) * (1.0 / EPS), tile)


def place_right(w, parts):
    width = parts[0].shape[1]
    for o, part in enumerate(parts):
        h = o % 2
        w[o // 2, h * HALF : (h + 1) * HALF, h * width : (h + 1) * width] = part


def evaluate(lefts, w, width):
    sums = [0.0, 0.0, 0.0]
    total = w.shape[2] // 2
    for start in range(0, total, width):
        if width == total:
            wide = [
                jnp.dot(lefts[p], w[p], preferred_element_type=F32) for p in range(2)
            ]
            found = [v[:, h * width : (h + 1) * width] for v in wide for h in range(2)]
        else:
            found = [
                jnp.dot(
                    lefts[o // 2],
                    w[o // 2, :, o % 2 * total + start : o % 2 * total + start + width],
                    preferred_element_type=F32,
                )
                for o in range(4)
            ]
        u = lax.rsqrt(found[0])
        cube = u * u * u
        for c in range(3):
            product = cube * found[1 + c]
            for j in range(0, width, 128):
                sums[c] = sums[c] + product[:, j : j + 128]
    return [jnp.sum(s, axis=1, keepdims=True) for s in sums]


def near_kernel(n_blocks, which, last, groups, n_far, slots, *refs):
    list_ref, cen_ref = refs[:2]
    blocks = refs[2 : 2 + n_blocks]
    refs = refs[2 + n_blocks :]
    left_ref, upw_ref = refs[:2]
    refs = refs[2:]
    if last:
        cols_in, tail_in, self_ref = refs[:3]
        far_refs = refs[3 : 3 + n_far]
        out_ref = refs[3 + n_far]
        pool, fine, tails, cols, wa, wb, wt = refs[4 + n_far :]
    else:
        cols, tails, pool, fine, wa, wb = refs

    rows = left_ref.shape[0]
    points = left_ref.shape[2]
    full = upw_ref.shape[1] - 128
    held = blocks[0].shape[0] // (LINES * rows) * (LINES * rows)
    for i, block in enumerate(blocks):
        pool[pl.ds(i * held, held), :] = block[:held, :]
    pool[pl.ds(n_blocks * held, 16), :] = jnp.zeros((16, 128), F32)
    wa[...] = jnp.zeros_like(wa)
    wb[...] = jnp.zeros_like(wb)
    if last:
        wt[...] = jnp.zeros_like(wt)
        cols[...] = cols_in[...]
        tails[...] = tail_in[...]
    else:
        cols[...] = jnp.zeros_like(cols)
        tails[...] = jnp.zeros_like(tails)

    n = list_ref[which, list_ref.shape[1] - 1]
    sub = iota((8, 128), 0)
    lane = iota((8, 128), 1)
    body = sub % 4 < 3
    tail = points - 128
    own_lanes = jnp.logical_and(lane // tail == sub, body)
    part = iota((8 * BATCH, 128), 1) // tail
    k_lane = lane // (128 // slots)

    def center_of(t):
        return [cen_ref[c, t] for c in range(3)]

    def upsample(b, _):
        tiles = [
            pool[pl.ds(LINES * spot_of(list_ref[which, b * BATCH + j]), 8), :]
            for j in range(BATCH)
        ]
        heads = jnp.concatenate([jnp.where(body, v, 0.0) for v in tiles], axis=0)
        ends = jnp.concatenate([jnp.where(own_lanes, v[3:4, :], 0.0) for v in tiles], axis=0)
        reach = tail
        while reach < 128:
            ends = ends + pltpu.roll(ends, reach, 1)
            reach *= 2
        h, m, l = split3(ends)
        ends = jnp.where(part == 2, l, jnp.where(jnp.logical_or(part == 1, part == 4), m, h))
        wide = jnp.concatenate([stack_left(heads, 1), ends], axis=1).astype(BF16)
        out = jnp.dot(wide, upw_ref[...], preferred_element_type=F32)
        out = out.reshape(BATCH, 8, full + 128)
        for j in range(BATCH):
            i = b * BATCH + j
            code = list_ref[which, i]
            t = target_of(code)
            center = center_of(t)
            fine[i] = shifted(out[j, :, :full], center)
            mine = jnp.logical_and(k_lane == slot_of(code), i < n)
            tails[t] = jnp.where(mine, shifted(out[j, :, full:], center), tails[t])
        return 0

    lax.fori_loop(0, (n + BATCH - 1) // BATCH, upsample, 0)

    lane_p = iota((points, 128), 1)

    def add_cols(found):
        for c in range(3):
            value = cols[c]
            for t, sums in found:
                value = value + jnp.where(lane_p == t, sums[c], 0.0)
            cols[c] = value

    def build(i, w):
        for j in range(UNITS):
            place_right(w.at[j], right(fine.at[i * UNITS + j]))

    def main(i, w):
        found = []
        for j in range(UNITS):
            t = target_of(list_ref[which, i * UNITS + j])
            lefts = [left_ref[t, p, :, : 2 * HALF] for p in range(2)]
            found.append((t, evaluate(lefts, w.at[j], 256)))
        add_cols(found)

    build(0, wa)

    def two(i, _):
        build(2 * i + 1, wb)
        main(2 * i, wa)
        build(2 * i + 2, wa)
        main(2 * i + 1, wb)
        return 0

    lax.fori_loop(0, (n + 2 * UNITS - 1) // (2 * UNITS), two, 0)

    if last:

        def tail_pass(i, _):
            found = []
            for j in range(TAILS):
                t = i * TAILS + j
                place_right(wt.at[j], right(tails.at[t]))
                lefts = [left_ref[t, p, :, : 2 * HALF] for p in range(2)]
                found.append((t, evaluate(lefts, wt.at[j], 128)))
            for c in range(3):
                value = jnp.zeros((points, 128), F32)
                for t, sums in found:
                    value = jnp.where(lane_p == t, sums[c], value)
                cols[c] += value
            return 0

        lax.fori_loop(0, rows // TAILS, tail_pass, 0)
        far = far_sums(groups, rows, far_refs)
        for c in range(3):
            turned = jnp.transpose(cols[c])[:rows]
            out_ref[c] = turned * (1.0 / EPS) + self_ref[c] + far[c]


def near(which, last, groups, blocks, lists, cen, lefts, upw, extra, far=()):
    rows, _, points, _ = lefts.shape
    full = upw.shape[1] - 128
    n_blocks = len(blocks)
    size = lists.shape[1] - 1
    slots = (size - PADS) // rows
    cols = jax.ShapeDtypeStruct((3, points, 128), F32)
    tails = jax.ShapeDtypeStruct((rows, 8, 128), F32)
    if last:
        out_shape = jax.ShapeDtypeStruct((3, rows, points), F32)
        out_specs = VMEM_SPEC
    else:
        out_shape = (cols, tails)
        out_specs = (VMEM_SPEC, VMEM_SPEC)
    scratch = [
        pltpu.VMEM((n_blocks * (blocks[0].shape[0] // (LINES * rows) * (LINES * rows)) + 16, 128), F32),
        pltpu.VMEM((size, 8, full), F32),
    ]
    if last:
        scratch += [pltpu.VMEM(tails.shape, F32), pltpu.VMEM(cols.shape, F32)]
    scratch += [pltpu.VMEM((UNITS, 2, 2 * HALF, 2 * full), BF16)] * 2
    if last:
        scratch += [pltpu.VMEM((TAILS, 2, 2 * HALF, 256), BF16)]
    n_vmem = n_blocks + 2 + len(extra) + len(far)
    return pl.pallas_call(
        functools.partial(near_kernel, n_blocks, which, last, groups, len(far), slots),
        out_shape=out_shape,
        in_specs=[SMEM_SPEC] * 2 + [VMEM_SPEC] * n_vmem,
        out_specs=out_specs,
        scratch_shapes=scratch,
        compiler_params=params(44),
        cost_estimate=cost(25 if last else 0.3),
        name="near_last" if last else "near_own",
    )(lists, cen, *blocks, lefts, upw, *extra, *far)


def far_sums(groups, rows, refs):
    domain = lax.axis_index("domain")
    group = lax.axis_index("group")
    block = refs[0][0][:, :rows]
    center = [column(block[c : c + 1]) for c in range(3)]
    leaf = column(block[6:7])
    leaves = jnp.concatenate(
        [refs[0][jnp.bitwise_xor(group, g)][:, rows : rows + 8] for g in range(groups)], axis=0
    )
    count = groups * 8
    first = (domain * count).astype(F32)
    hot = (leaf - first == iota((rows, count), 1).astype(F32)).astype(F32)
    lists = jnp.dot(hot, leaves, precision=HIGHEST, preferred_element_type=F32)
    lists = jnp.round(lists)
    wanted = [jnp.broadcast_to(lists[:, k : k + 1], (rows, 128)) for k in range(8)]
    lane = iota((8, 128), 1)

    def one(ref, i, sums):
        both = jnp.where(lane < rows, ref[2 * i], pltpu.roll(ref[2 * i + 1], rows, 1))
        rel = [center[c] - both[c : c + 1] for c in range(3)]
        force = [both[3 + c : 4 + c] for c in range(3)]
        source = both[6:7]
        times = jnp.zeros((rows, 128), F32)
        for k in range(8):
            times = times + jnp.where(wanted[k] == source, 1.0, 0.0)
        dist = rel[0] * rel[0] + rel[1] * rel[1] + rel[2] * rel[2] + EPS * EPS
        u = lax.rsqrt(dist)
        u3 = u * u * u * times
        near_part = (dist + EPS * EPS) * u3
        project = (rel[0] * force[0] + rel[1] * force[1] + rel[2] * force[2]) * u3
        return [sums[c] + near_part * force[c] + project * rel[c] for c in range(3)]

    sums = [jnp.zeros((rows, 128), F32)] * 3
    for ref in refs:
        sums = lax.fori_loop(0, ref.shape[0] // 2, functools.partial(one, ref), sums, unroll=min(4, ref.shape[0] // 2))
    return [jnp.sum(v, axis=1, keepdims=True) for v in sums]


def swap(x, axis, bit):
    return lax.ppermute(x, axis, [(i, i ^ bit) for i in range(lax.axis_size(axis))])


def bits(n):
    found = []
    bit = 1
    while bit < n:
        found.append(bit)
        bit *= 2
    return found


def shards(
    centers,
    offsets,
    density,
    area,
    upsample,
    self_operator,
    near_sources,
    near_counts,
    leaf_slot,
    leaf_list,
):
    rows = centers.shape[0]
    groups = lax.axis_size("group")
    domains = lax.axis_size("domain")
    cen = centers.T
    off = jnp.transpose(offsets, (1, 0, 2))
    den = jnp.transpose(density, (1, 0, 2))
    tiles = pack(cen, off, den, area, leaf_slot[None, :], leaf_list)
    held = LINES * rows
    ends = domains - 1
    above = lax.ppermute(tiles, "domain", [(i + 1, i) for i in range(ends)])
    below = lax.ppermute(tiles, "domain", [(i, i + 1) for i in range(ends)])
    own = by_group(tiles, groups)

    lefts, lists = left(groups, near_sources.T, near_counts[None, :], off)
    own, den = after((own, den), (lefts,))
    below, above = after((below, above), (lefts,))
    both = jnp.concatenate([below[:held], above[:held]], axis=0)
    far = [jnp.concatenate([v[held:].reshape(1, 8, 128) for v in own], axis=0)]
    hops = []
    steps = bits(domains)
    self_term = None
    for turn in range(max(len(steps), groups - 1)):
        if turn < len(steps):
            far.append(swap(jnp.concatenate(far, axis=0), "domain", steps[turn]))
        if turn + 1 < groups:
            hops.append(swap(both, "group", turn + 1))
        if turn == 0:
            self_term, upw = setup(den, self_operator, upsample.T)
            far = after(far, (self_term,))
    sides = [both] + hops
    lists = after(lists, far[:-1])
    cols, tails = near(0, False, groups, own, lists, cen, lefts, upw, ())
    out = near(
        1, True, groups, sides, lists, cen, lefts, upw, (cols, tails, self_term), far
    )
    return jnp.transpose(out, (1, 0, 2))


def after(values, others):
    return lax.optimization_barrier((values, others))[0]


def by_group(block, groups):
    return [block] + [swap(block, "group", i) for i in range(1, groups)]


def combine(held, steps):
    whole = held[0] if len(held) == 1 else jnp.concatenate(held, axis=0)
    masks = [steps[0]] if len(steps) == 1 else [steps[0], steps[1], steps[0] ^ steps[1]]
    return [swap(whole, "domain", mask) for mask in masks]


def solution(mesh):
    in_specs = (
        P(("domain", "group"), None),
        P(("domain", "group"), None, None),
        P(("domain", "group"), None, None),
        P(("domain", "group"), None),
        P(),
        P(),
        P(("domain", "group"), None),
        P(("domain", "group")),
        P(("domain", "group")),
        P(("domain", "group"), None),
    )
    out_specs = P(("domain", "group"), None, None)
    return jax.shard_map(shards, mesh=mesh, in_specs=in_specs, out_specs=out_specs, check_vma=False)
```

```python
import functools

import jax
import jax.numpy as jnp
from jax import lax
from jax.experimental import pallas as pl
from jax.experimental.pallas import tpu as pltpu
from jax.sharding import PartitionSpec as P

LEAF_CAP = 16
EPS = 0.5
UNITS = 8
BATCH = 32
TAILS = 16
LINES = 7
PADS = BATCH + 2 * UNITS
HALF = 48
F32 = jnp.float32
BF16 = jnp.bfloat16
HIGHEST = lax.Precision.HIGHEST
VMEM_SPEC = pl.BlockSpec(memory_space=pltpu.VMEM)
SMEM_SPEC = pl.BlockSpec(memory_space=pltpu.SMEM)


def params(mib=60):
    return pltpu.CompilerParams(vmem_limit_bytes=mib << 20)


def cost(micros):
    return pl.CostEstimate(
        flops=int(micros * 1e9), bytes_accessed=int(micros * 3e6), transcendentals=0
    )


def iota(shape, dim):
    return lax.broadcasted_iota(jnp.int32, shape, dim)


def split3(value):
    high = value.astype(BF16).astype(F32)
    rest = value - high
    mid = rest.astype(BF16).astype(F32)
    return high, mid, rest - mid


def stack_left(value, axis):
    h, m, l = split3(value)
    return jnp.concatenate([h, m, l, h, m, h], axis=axis)


def stack_right(value, axis):
    h, m, l = split3(value)
    return jnp.concatenate([h, h, h, m, m, l], axis=axis)


def dot_nt(a, b, precision=None):
    return lax.dot_general(
        a, b, (((1,), (1,)), ((), ())), precision=precision, preferred_element_type=F32
    )


def column(row):
    n = row.shape[1]
    eye = iota((n, n), 0) == iota((n, n), 1)
    return jnp.sum(jnp.where(eye, row, jnp.zeros_like(row)), axis=1, keepdims=True)


def as_row(col):
    n = col.shape[0]
    eye = iota((n, n), 0) == iota((n, n), 1)
    return jnp.sum(jnp.where(eye, col, jnp.zeros_like(col)), axis=0, keepdims=True)


def pack_kernel(cen_ref, off_ref, den_ref, area_ref, leaf_ref, list_ref, tile_ref):
    rows, points = area_ref.shape
    area = area_ref[...]
    tail = points - 128
    tails = []
    lines = []
    for c in range(3):
        grid = off_ref[c] + column(cen_ref[c : c + 1, :])
        tile_ref[pl.ds(c, rows, LINES), :] = grid[:, :128]
        tails.append(grid[:, 128:])
    tails.append(jnp.zeros((rows, tail), F32))
    for c in range(3):
        weighted = den_ref[c] * area
        tile_ref[pl.ds(4 + c, rows, LINES), :] = weighted[:, :128]
        tails.append(weighted[:, 128:])
        lines.append(as_row(jnp.sum(weighted, axis=1, keepdims=True)))
    tails.append(jnp.zeros((rows, tail), F32))
    tile_ref[pl.ds(3, rows, LINES), :] = jnp.concatenate(tails, axis=1)
    leaf = (leaf_ref[...] // LEAF_CAP).astype(F32)
    block = jnp.concatenate([cen_ref[...]] + lines + [leaf, jnp.zeros((1, rows), F32)], axis=0)
    lists = list_ref[...].astype(F32)
    rest = 128 - rows - lists.shape[1]
    tile_ref[LINES * rows :, :] = jnp.concatenate([block, lists, jnp.zeros((8, rest), F32)], axis=1)


def pack(cen, off, den, area, leaf, lists):
    rows = area.shape[0]
    return pl.pallas_call(
        pack_kernel,
        out_shape=jax.ShapeDtypeStruct((LINES * rows + 8, 128), F32),
        in_specs=[VMEM_SPEC] * 6,
        out_specs=VMEM_SPEC,
        compiler_params=params(),
        cost_estimate=cost(2),
        name="pack",
    )(cen, off, den, area, leaf, lists)


def quotient(value, by):
    if by & (by - 1) == 0:
        return lax.shift_right_logical(value, by.bit_length() - 1), jnp.bitwise_and(value, by - 1)
    return lax.div(value, by), lax.rem(value, by)


def encode(spot, slot, target):
    return spot * (1 << 12) + slot * (1 << 8) + target


def target_of(code):
    return jnp.bitwise_and(code, (1 << 8) - 1)


def slot_of(code):
    return jnp.bitwise_and(lax.shift_right_logical(code, 8), 15)


def spot_of(code):
    return lax.shift_right_logical(code, 12)


def add_pairs(groups, src_ref, cnt_ref, list_ref, t, ends):
    slots, rows = src_ref.shape
    domain = lax.axis_index("domain")
    group = lax.axis_index("group")
    live = cnt_ref[0, t]
    ends = list(ends)
    for k in range(slots):
        device, local = quotient(src_ref[k, t], rows)
        home, turn = quotient(device, groups)
        step = home - domain
        here = step == 0
        held = jnp.where(here, rows, 2 * rows)
        spot = jnp.bitwise_xor(turn, group) * held + local + jnp.where(step > 0, rows, 0)
        list_ref[jnp.where(here, 0, 1), jnp.where(here, ends[0], ends[1])] = encode(spot, k, t)
        is_live = k < live
        ends[0] += jnp.where(jnp.logical_and(is_live, here), 1, 0)
        ends[1] += jnp.where(jnp.logical_and(is_live, jnp.logical_not(here)), 1, 0)
    return tuple(ends)


def end_lists(block, list_ref, ends):
    width = list_ref.shape[1]
    for which in range(2):
        list_ref[which, width - 1] = ends[which]
        for i in range(PADS):
            list_ref[which, ends[which] + i] = encode((which + 1) * block, 0, 0)


def setup_kernel(den_ref, op_ref, up_ref, self_ref, upw_ref):
    points = den_ref.shape[2]
    for c in range(3):
        self_ref[c] = dot_nt(den_ref[c], op_ref[...], HIGHEST)

    fine = up_ref.shape[1]
    full = fine // 128 * 128
    rest = fine - full
    tail = points - 128
    up = up_ref[...]
    wide = jnp.concatenate([up[:, :full]] + [up[:, full:]] * (128 // rest), axis=1)
    spare = jnp.zeros((128 - 6 * tail, full + 128), F32)
    upw_ref[...] = jnp.concatenate(
        [stack_right(wide[:128], 0), stack_right(wide[128:], 0), spare], axis=0
    ).astype(BF16)


def setup(den, op, up_t):
    fine = up_t.shape[1]
    return pl.pallas_call(
        setup_kernel,
        out_shape=(
            jax.ShapeDtypeStruct(den.shape, F32),
            jax.ShapeDtypeStruct((6 * 128 + 128, fine // 128 * 128 + 128), BF16),
        ),
        in_specs=[VMEM_SPEC] * 3,
        out_specs=(VMEM_SPEC,) * 2,
        compiler_params=params(24),
        cost_estimate=cost(5),
        name="setup",
    )(den, op, up_t)


def left_kernel(groups, src_ref, cnt_ref, off_ref, left_ref, list_ref):
    _, rows, points = off_ref.shape
    eye = (iota((points, points), 0) == iota((points, points), 1)).astype(BF16)

    def one_left(t):
        x = [off_ref[c, pl.ds(t, 1), :] * (1.0 / EPS) for c in range(3)]
        xx = x[0] * x[0] + x[1] * x[1] + x[2] * x[2]
        one = jnp.ones_like(xx)
        zero = jnp.zeros_like(xx)
        cases = [x + [one, xx, zero, zero, zero]]
        for c in range(3):
            extra = [x[c] * x[b] for b in range(3)]
            extra[c] = extra[c] + xx
            cases.append(x + [one] + extra + [zero])
        stacked = [stack_left(jnp.concatenate(v, axis=0), 0) for v in cases]
        for p in range(2):
            both = jnp.concatenate(stacked[2 * p : 2 * p + 2], axis=0).astype(BF16)
            left_ref[t, p, :, : 2 * HALF] = dot_nt(eye, both).astype(BF16)

    each = 8

    def some_left(i, ends):
        for j in range(each):
            ends = add_pairs(groups, src_ref, cnt_ref, list_ref, i * each + j, ends)
            one_left(i * each + j)
        return ends

    ends = lax.fori_loop(0, rows // each, some_left, (0, 0))
    end_lists(groups * rows, list_ref, ends)


def left(groups, src, cnt, off):
    _, rows, points = off.shape
    return pl.pallas_call(
        functools.partial(left_kernel, groups),
        out_shape=(
            jax.ShapeDtypeStruct((rows, 2, points, 128), BF16),
            jax.ShapeDtypeStruct((2, src.shape[0] * rows + PADS + 1), jnp.int32),
        ),
        in_specs=[SMEM_SPEC] * 2 + [VMEM_SPEC],
        out_specs=(VMEM_SPEC, SMEM_SPEC),
        compiler_params=params(24),
        cost_estimate=cost(10),
        name="left",
    )(src, cnt, off)


def right(ref):
    tile = ref[...]
    sub = iota(tile.shape, 0)
    y = [ref[c : c + 1, :] for c in range(3)]
    f = [ref[4 + c : 5 + c, :] for c in range(3)]
    yy = y[0] * y[0] + y[1] * y[1] + y[2] * y[2]
    yf = y[0] * f[0] + y[1] * f[1] + y[2] * f[2]
    rest = jnp.where(sub < 4, 0.0, tile)
    points = jnp.where(sub < 3, -2.0 * tile, jnp.where(sub == 3, yy + 2.0, 0.0))
    forces = jnp.where(sub < 3, -pltpu.roll(tile, 4, 0), jnp.where(sub == 3, yf, 0.0))
    outs = [points + jnp.where(sub == 3, -1.0, jnp.where(sub == 4, 1.0, 0.0))]
    for c in range(3):
        outs.append(f[c] * points + y[c] * forces + jnp.where(sub == c, -yf, rest))
    return [stack_right(v, 0).astype(BF16) for v in outs]


def shifted(tile, center):
    sub = iota(tile.shape, 0)
    shift = jnp.where(sub == 0, center[0], jnp.where(sub == 1, center[1], center[2]))
    return jnp.where(sub < 3, (tile - shift) * (1.0 / EPS), tile)


def place_right(w, parts):
    width = parts[0].shape[1]
    for o, part in enumerate(parts):
        h = o % 2
        w[o // 2, h * HALF : (h + 1) * HALF, h * width : (h + 1) * width] = part


def clear(w):
    count, pairs, lines, lanes = w.shape
    zero = jnp.zeros((count, pairs, lines // 2, lanes // 2), BF16)
    w[:, :, : lines // 2, lanes // 2 :] = zero
    w[:, :, lines // 2 :, : lanes // 2] = zero


def evaluate(lefts, w, width):
    sums = [0.0, 0.0, 0.0]
    total = w.shape[2] // 2
    for start in range(0, total, width):
        if width == total:
            wide = [
                jnp.dot(lefts[p], w[p], preferred_element_type=F32) for p in range(2)
            ]
            found = [v[:, h * width : (h + 1) * width] for v in wide for h in range(2)]
        else:
            found = [
                jnp.dot(
                    lefts[o // 2],
                    w[o // 2, :, o % 2 * total + start : o % 2 * total + start + width],
                    preferred_element_type=F32,
                )
                for o in range(4)
            ]
        u = lax.rsqrt(found[0])
        cube = u * u * u
        for c in range(3):
            product = cube * found[1 + c]
            for j in range(0, width, 128):
                sums[c] = sums[c] + product[:, j : j + 128]
    return [jnp.sum(s, axis=1, keepdims=True) for s in sums]


def near_kernel(n_blocks, which, last, slots, *refs):
    list_ref, cen_ref = refs[:2]
    blocks = refs[2 : 2 + n_blocks]
    refs = refs[2 + n_blocks :]
    left_ref, upw_ref = refs[:2]
    refs = refs[2:]
    if last:
        cols_in, tail_in, self_ref, far_ref, out_ref = refs[:5]
        pool, fine, tails, cols, wa, wb, wt = refs[5:]
    else:
        cols, tails, pool, fine, wa, wb = refs

    rows = left_ref.shape[0]
    points = left_ref.shape[2]
    full = upw_ref.shape[1] - 128
    held = blocks[0].shape[0] // (LINES * rows) * (LINES * rows)
    for i, block in enumerate(blocks):
        pool[pl.ds(i * held, held), :] = block[:held, :]
    pool[pl.ds(n_blocks * held, 16), :] = jnp.zeros((16, 128), F32)
    clear(wa)
    clear(wb)
    if last:
        clear(wt)
        cols[...] = cols_in[...]
        tails[...] = tail_in[...]
    else:
        cols[...] = jnp.zeros_like(cols)
        tails[...] = jnp.zeros_like(tails)

    n = list_ref[which, list_ref.shape[1] - 1]
    sub = iota((8, 128), 0)
    lane = iota((8, 128), 1)
    body = sub % 4 < 3
    tail = points - 128
    own_lanes = jnp.logical_and(lane // tail == sub, body)
    part = iota((8 * BATCH, 128), 1) // tail
    k_lane = lane // (128 // slots)

    def center_of(t):
        return [cen_ref[c, t] for c in range(3)]

    def upsample(b, _):
        tiles = [
            pool[pl.ds(LINES * spot_of(list_ref[which, b * BATCH + j]), 8), :]
            for j in range(BATCH)
        ]
        heads = jnp.concatenate([jnp.where(body, v, 0.0) for v in tiles], axis=0)
        ends = jnp.concatenate([jnp.where(own_lanes, v[3:4, :], 0.0) for v in tiles], axis=0)
        reach = tail
        while reach < 128:
            ends = ends + pltpu.roll(ends, reach, 1)
            reach *= 2
        h, m, l = split3(ends)
        ends = jnp.where(part == 2, l, jnp.where(jnp.logical_or(part == 1, part == 4), m, h))
        wide = jnp.concatenate([stack_left(heads, 1), ends], axis=1).astype(BF16)
        out = jnp.dot(wide, upw_ref[...], preferred_element_type=F32)
        out = out.reshape(BATCH, 8, full + 128)
        for j in range(BATCH):
            i = b * BATCH + j
            code = list_ref[which, i]
            t = target_of(code)
            center = center_of(t)
            fine[i] = shifted(out[j, :, :full], center)
            mine = jnp.logical_and(k_lane == slot_of(code), i < n)
            tails[t] = jnp.where(mine, shifted(out[j, :, full:], center), tails[t])
        return 0

    lax.fori_loop(0, (n + BATCH - 1) // BATCH, upsample, 0)

    lane_p = iota((points, 128), 1)

    def add_cols(found):
        for c in range(3):
            value = cols[c]
            for t, sums in found:
                value = value + jnp.where(lane_p == t, sums[c], 0.0)
            cols[c] = value

    def build(i, w):
        for j in range(UNITS):
            place_right(w.at[j], right(fine.at[i * UNITS + j]))

    def main(i, w):
        found = []
        for j in range(UNITS):
            t = target_of(list_ref[which, i * UNITS + j])
            lefts = [left_ref[t, p, :, : 2 * HALF] for p in range(2)]
            found.append((t, evaluate(lefts, w.at[j], 256)))
        add_cols(found)

    build(0, wa)

    def two(i, _):
        build(2 * i + 1, wb)
        main(2 * i, wa)
        build(2 * i + 2, wa)
        main(2 * i + 1, wb)
        return 0

    lax.fori_loop(0, (n + 2 * UNITS - 1) // (2 * UNITS), two, 0)

    if last:

        def tail_pass(i, _):
            found = []
            for j in range(TAILS):
                t = i * TAILS + j
                place_right(wt.at[j], right(tails.at[t]))
                lefts = [left_ref[t, p, :, : 2 * HALF] for p in range(2)]
                found.append((t, evaluate(lefts, wt.at[j], 128)))
            for c in range(3):
                value = jnp.zeros((points, 128), F32)
                for t, sums in found:
                    value = jnp.where(lane_p == t, sums[c], value)
                cols[c] += value
            return 0

        lax.fori_loop(0, rows // TAILS, tail_pass, 0)
        for c in range(3):
            turned = jnp.transpose(cols[c])[:rows]
            out_ref[c] = turned * (1.0 / EPS) + self_ref[c] + far_ref[c][:, :1]


def near(which, last, blocks, lists, cen, lefts, upw, extra):
    rows, _, points, _ = lefts.shape
    full = upw.shape[1] - 128
    n_blocks = len(blocks)
    size = lists.shape[1] - 1
    slots = (size - PADS) // rows
    cols = jax.ShapeDtypeStruct((3, points, 128), F32)
    tails = jax.ShapeDtypeStruct((rows, 8, 128), F32)
    if last:
        out_shape = jax.ShapeDtypeStruct((3, rows, points), F32)
        out_specs = VMEM_SPEC
    else:
        out_shape = (cols, tails)
        out_specs = (VMEM_SPEC, VMEM_SPEC)
    scratch = [
        pltpu.VMEM((n_blocks * (blocks[0].shape[0] // (LINES * rows) * (LINES * rows)) + 16, 128), F32),
        pltpu.VMEM((size, 8, full), F32),
    ]
    if last:
        scratch += [pltpu.VMEM(tails.shape, F32), pltpu.VMEM(cols.shape, F32)]
    scratch += [pltpu.VMEM((UNITS, 2, 2 * HALF, 2 * full), BF16)] * 2
    if last:
        scratch += [pltpu.VMEM((TAILS, 2, 2 * HALF, 256), BF16)]
    n_vmem = n_blocks + 2 + len(extra)
    return pl.pallas_call(
        functools.partial(near_kernel, n_blocks, which, last, slots),
        out_shape=out_shape,
        in_specs=[SMEM_SPEC] * 2 + [VMEM_SPEC] * n_vmem,
        out_specs=out_specs,
        scratch_shapes=scratch,
        compiler_params=params(44),
        cost_estimate=cost(25 if last else 0.3),
        name="near_last" if last else "near_own",
    )(lists, cen, *blocks, lefts, upw, *extra)


def far_field(groups, rows, loads):
    return pl.pallas_call(
        functools.partial(far_kernel, groups),
        out_shape=jax.ShapeDtypeStruct((3, rows, 128), F32),
        in_specs=[VMEM_SPEC] * len(loads),
        out_specs=VMEM_SPEC,
        compiler_params=params(24),
        cost_estimate=cost(2),
        name="far",
    )(*loads)


def far_kernel(groups, *refs):
    *refs, far_ref = refs
    rows = far_ref.shape[1]
    domain = lax.axis_index("domain")
    group = lax.axis_index("group")
    block = refs[0][0][:, :rows]
    center = [column(block[c : c + 1]) for c in range(3)]
    leaf = column(block[6:7])
    leaves = jnp.concatenate(
        [refs[0][jnp.bitwise_xor(group, g)][:, rows : rows + 8] for g in range(groups)], axis=0
    )
    count = groups * 8
    first = (domain * count).astype(F32)
    hot = (leaf - first == iota((rows, count), 1).astype(F32)).astype(F32)
    lists = jnp.dot(hot, leaves, precision=HIGHEST, preferred_element_type=F32)
    lists = jnp.round(lists)
    wanted = [jnp.broadcast_to(lists[:, k : k + 1], (rows, 128)) for k in range(8)]
    lane = iota((8, 128), 1)

    def one(ref, i, sums):
        both = jnp.where(lane < rows, ref[2 * i], pltpu.roll(ref[2 * i + 1], rows, 1))
        rel = [center[c] - both[c : c + 1] for c in range(3)]
        force = [both[3 + c : 4 + c] for c in range(3)]
        source = both[6:7]
        times = jnp.zeros((rows, 128), F32)
        for k in range(8):
            times = times + jnp.where(wanted[k] == source, 1.0, 0.0)
        dist = rel[0] * rel[0] + rel[1] * rel[1] + rel[2] * rel[2] + EPS * EPS
        u = lax.rsqrt(dist)
        u3 = u * u * u * times
        near_part = (dist + EPS * EPS) * u3
        project = (rel[0] * force[0] + rel[1] * force[1] + rel[2] * force[2]) * u3
        return [sums[c] + near_part * force[c] + project * rel[c] for c in range(3)]

    sums = [jnp.zeros((rows, 128), F32)] * 3
    for ref in refs:
        sums = lax.fori_loop(0, ref.shape[0] // 2, functools.partial(one, ref), sums, unroll=min(4, ref.shape[0] // 2))
    for c in range(3):
        far_ref[c] = jnp.broadcast_to(jnp.sum(sums[c], axis=1, keepdims=True), (rows, 128))


def swap(x, axis, bit):
    return lax.ppermute(x, axis, [(i, i ^ bit) for i in range(lax.axis_size(axis))])


def bits(n):
    found = []
    bit = 1
    while bit < n:
        found.append(bit)
        bit *= 2
    return found


def shards(
    centers,
    offsets,
    density,
    area,
    upsample,
    self_operator,
    near_sources,
    near_counts,
    leaf_slot,
    leaf_list,
):
    rows = centers.shape[0]
    groups = lax.axis_size("group")
    domains = lax.axis_size("domain")
    cen = centers.T
    off = jnp.transpose(offsets, (1, 0, 2))
    den = jnp.transpose(density, (1, 0, 2))
    tiles = pack(cen, off, den, area, leaf_slot[None, :], leaf_list)
    held = LINES * rows
    ends = domains - 1
    above = lax.ppermute(tiles, "domain", [(i + 1, i) for i in range(ends)])
    below = lax.ppermute(tiles, "domain", [(i, i + 1) for i in range(ends)])
    own = by_group(tiles, groups)

    lefts, lists = left(groups, near_sources.T, near_counts[None, :], off)
    own, den = after((own, den), (lefts,))
    steps = bits(domains)
    far = [jnp.concatenate([v[held:].reshape(1, 8, 128) for v in own], axis=0)]
    far.append(swap(far[0], "domain", steps[0]))
    below, above = after((below, above), (far,))
    both = jnp.concatenate([below[:held], above[:held]], axis=0)
    sides = by_group(both, groups)
    self_term, upw = setup(den, self_operator, upsample.T)
    for step in steps[1:]:
        far.append(swap(jnp.concatenate(far, axis=0), "domain", step))
    lists = after(lists, far[:-1])
    cols, tails = near(0, False, own, lists, cen, lefts, upw, ())
    far, cols = after((far, cols), (cols,))
    out = near(
        1, True, sides, lists, cen, lefts, upw,
        (cols, tails, self_term, far_field(groups, rows, far)),
    )
    return jnp.transpose(out, (1, 0, 2))


def after(values, others):
    return lax.optimization_barrier((values, others))[0]


def by_group(block, groups):
    return [block] + [swap(block, "group", i) for i in range(1, groups)]


def combine(held, steps):
    whole = held[0] if len(held) == 1 else jnp.concatenate(held, axis=0)
    masks = [steps[0]] if len(steps) == 1 else [steps[0], steps[1], steps[0] ^ steps[1]]
    return [swap(whole, "domain", mask) for mask in masks]


def solution(mesh):
    in_specs = (
        P(("domain", "group"), None),
        P(("domain", "group"), None, None),
        P(("domain", "group"), None, None),
        P(("domain", "group"), None),
        P(),
        P(),
        P(("domain", "group"), None),
        P(("domain", "group")),
        P(("domain", "group")),
        P(("domain", "group"), None),
    )
    out_specs = P(("domain", "group"), None, None)
    return jax.shard_map(shards, mesh=mesh, in_specs=in_specs, out_specs=out_specs, check_vma=False)
```
